512 devices in a mesh: pool: 16 (over x_hi, z), comp: 32 (over y, x_lo, core).
Axes of the slice: x: 4 (x_hi: 2, x_lo: 2; x = x_hi * 2 + x_lo), y: 8, z: 8, core: 2. Of those that a mesh axis runs over, the one named last changes fastest.
Arguments:
- queries: bfloat16 [16, 1024, 8192], P('pool', None, 'comp'), may hold values from -512 to 512
- fresh_kv: bfloat16 [16, 1024, 32, 256], P('pool', None, 'comp'), may hold values from -8 to 8, as said below
- head_hidden: bfloat16 [16, 128, 8192], P('pool', None, 'comp'), may hold values from -4096 to 4096
- norm_gain: bfloat16 [8192], P('comp'), may hold values from 0.5 to 1.5
- kv_weight: bfloat16 [8192, 2048], P('comp'), may hold values from -0.0625 to 0.0625
- kv_store: bfloat16 [1024, 64, 32, 256], P('pool', None, 'comp'), may hold values from -8 to 8, as said below
- split_blocks: int32 [16], P('pool'), may hold values from 0 to 2
- tail_counts: int32 [16], replicated, may hold values from 32 to 64, as said below
- holder_list: int32 [16, 64], replicated, may hold values from 0 to 15, as said below
- slot_list: int32 [16, 64], replicated, may hold values from 0 to 63, as said below
Outputs:
- attention_out: bfloat16 [16, 1024, 8192], P('pool', None, 'comp')
The draws below stay inside these ranges and needn't reach their ends.
Inputs may be any that keep to these rules, and one draw needn't show every extreme that they name: fresh_kv[:, :, r] is equal for all ranks r of one KV head, the head r // 4. kv_store[:, :, r] is equal for all ranks r of one KV head, as for fresh_kv. Slot b of holder h is row h * 64 + b. `tail_counts`: some session loads 64 blocks. `holder_list`: one holder holds at most 4 blocks of one session, and for every session some holder holds exactly 4 of its loaded blocks. `slot_list`: no two entries of any sessions share a holder and a slot.
All inputs are finite; a program needn't handle non-finite values.
Results may differ from the reference program's by a relative error of at most 0.0041.
Values may be sent and summed in bfloat16 or wider, within the bound.
No kernel may reach another device: no remote copies, remote signals or barrier semaphores. Data moves between devices by JAX's collectives and lax.ppermute only.
A program may use at most 64 MiB of HBM per device.

```python
import math
import jax
import jax.numpy as jnp
from jax import lax

D = 8192
QH = 64
KVH = 8
HD = 128
BLK = 64
HEADB = 2
TCELLS = 64
NEW = 1024
SESSIONS = 16
RANKS = 32
CAP = 4
STORE = 1024
N_POOL = 16


def fresh_base(key):
    base = jax.random.normal(jax.random.fold_in(key, 101), (SESSIONS, NEW, KVH, 2 * HD), jnp.float32)
    return base.at[:, 4:8, :, :HD].set(base[:, 4:8, :, :HD])


def cell_layout(key):

    def shuffle_pool(sub_key):
        return jax.random.permutation(sub_key, N_POOL).astype(jnp.int32)

    def shuffle_cells(sub_key):
        return jax.random.permutation(sub_key, TCELLS).astype(jnp.int32)
    holders_of = jax.vmap(shuffle_pool)(jax.random.split(jax.random.fold_in(key, 201), SESSIONS))
    shuffled = jax.vmap(shuffle_cells)(jax.random.split(jax.random.fold_in(key, 202), SESSIONS))
    leading = jax.random.randint(jax.random.fold_in(key, 203), (SESSIONS, 1), 0, N_POOL, dtype=jnp.int32)
    cell_ids = jnp.arange(TCELLS, dtype=jnp.int32)[None, :]
    priority = jnp.where(cell_ids % N_POOL == leading, cell_ids // N_POOL, shuffled + TCELLS)
    placed = jnp.argsort(priority, axis=1, stable=True).astype(jnp.int32)
    holder = jnp.take_along_axis(holders_of, placed % N_POOL, axis=1)
    slot_rows = jnp.arange(SESSIONS, dtype=jnp.int32)[:, None] * CAP + placed // N_POOL
    return (holder.astype(jnp.int32), slot_rows.astype(jnp.int32))


def draw_queries(key, part):
    key = jax.random.fold_in(key, 3)
    values = 2.5 * jax.random.normal(key, (SESSIONS, NEW, QH, HD), jnp.float32)
    return values.reshape(SESSIONS, NEW, QH * HD).astype(jnp.bfloat16)


def draw_fresh_kv(key, part):
    base = fresh_base(key)
    return jnp.repeat(base.astype(jnp.bfloat16), RANKS // KVH, axis=2)


def draw_head_hidden(key, part):
    key = jax.random.fold_in(key, 5)
    noise_key, row_key, col_key = jax.random.split(key, 3)
    full_shape = (SESSIONS, HEADB * BLK, D)
    trend_line = jnp.arange(D, dtype=jnp.float32) / D
    noise_part = jax.random.normal(noise_key, full_shape, jnp.float32)
    spread = math.log(10.0)
    slope_gain = 2.0
    row_scale = jnp.exp(jax.random.uniform(row_key, (SESSIONS, HEADB * BLK, 1), jnp.float32, 0.0, spread))
    col_scale = jnp.exp(jax.random.uniform(col_key, (D,), jnp.float32, 0.0, spread)) * (1.0 + slope_gain * trend_line)
    return (noise_part * row_scale * col_scale).astype(jnp.bfloat16)


def draw_kv_store(key, part):
    key = jax.random.fold_in(key, 9)
    full_shape = (STORE, BLK, KVH, 2 * HD)
    values = jax.random.normal(key, full_shape, jnp.float32)
    return jnp.repeat(values.astype(jnp.bfloat16), RANKS // KVH, axis=2)


def draw_tail_counts(key, part):
    key = jax.random.fold_in(key, 11)
    count_key, pick_key = jax.random.split(key, 2)
    counts = jax.random.randint(count_key, (SESSIONS,), TCELLS // 2, TCELLS + 1, dtype=jnp.int32)
    chosen = jax.random.randint(pick_key, (), 0, SESSIONS, dtype=jnp.int32)
    return jnp.where(jnp.arange(SESSIONS, dtype=jnp.int32) == chosen, TCELLS, counts).astype(jnp.int32)


def draw_holder_list(key, part):
    holder, slot_rows = cell_layout(key)
    return holder


def draw_slot_list(key, part):
    holder, slot_rows = cell_layout(key)
    return slot_rows


def set_ends(result, stream_key, smallest, largest):
    index_at = [jax.random.randint(jax.random.fold_in(stream_key, axis), (), 0, length) for axis, length in enumerate(result.shape)]
    widest = result.shape.index(max(result.shape))
    next_to = index_at[:widest] + [(index_at[widest] + 1) % result.shape[widest]] + index_at[widest + 1:]
    return result.at[tuple(index_at)].set(smallest).at[tuple(next_to)].set(largest)


def level_of(key, shape, shards, smallest, top_value):
    gain = 1.0
    for dim, blocks in shards:
        draws = jax.random.uniform(jax.random.fold_in(jax.random.fold_in(key, 6), dim), (blocks,), jnp.float32, smallest / len(shards), top_value / len(shards))
        gain = gain * jnp.repeat(jnp.exp(draws), shape[dim] // blocks).reshape((-1,) + (1,) * (len(shape) - 1 - dim))
    return gain


def scatter_about(key, dims, deviation, most, shards=(), held_as=jnp.bfloat16):
    values = jax.random.normal(key, dims, jnp.float32) * deviation
    if len(shards) > 0:
        values = level_of(key, dims, shards, -0.22, 0.18) * values
    return jnp.clip(values, min=-most, max=most).astype(held_as)


def setup_inputs(seed: int = 0) -> dict:
    splits = jax.random.split(jax.random.key(seed), 11)
    return {
        "queries": draw_queries(jax.random.fold_in(splits[10], 71), 0),
        "fresh_kv": draw_fresh_kv(jax.random.fold_in(splits[10], 71), 0),
        "head_hidden": draw_head_hidden(jax.random.fold_in(splits[10], 71), 0),
        "norm_gain": jnp.clip(1.0 + 0.1 * jax.random.normal(splits[3], (D,), jnp.float32), 0.5, 1.5).astype(jnp.bfloat16),
        "kv_weight": scatter_about(splits[4], (D, KVH * 2 * HD), D ** -0.5, 0.0625, ((0, 32),)),
        "kv_store": draw_kv_store(jax.random.fold_in(splits[10], 71), 0),
        "split_blocks": set_ends(jax.random.randint(splits[6], (SESSIONS,), 0, HEADB + 1), jax.random.fold_in(splits[6], 1), 0, HEADB).astype(jnp.int32),
        "tail_counts": draw_tail_counts(jax.random.fold_in(splits[10], 71), 0),
        "holder_list": draw_holder_list(jax.random.fold_in(splits[10], 71), 0),
        "slot_list": draw_slot_list(jax.random.fold_in(splits[10], 71), 0),
    }


def rotate_keys(key_rows, positions):
    half_dim = key_rows.shape[-1] // 2
    frequency = 500000.0 ** (-2.0 * jnp.arange(half_dim, dtype=jnp.float32) / key_rows.shape[-1])
    angles = positions.astype(jnp.float32)[:, None] * frequency[None, :]
    cosine = jnp.cos(angles)[:, None, :]
    sine_part = jnp.sin(angles)[:, None, :]
    first_half = key_rows[..., :half_dim]
    second = key_rows[..., half_dim:]
    return jnp.concatenate([first_half * cosine - second * sine_part, second * cosine + first_half * sine_part], axis=-1)

def reference(queries, fresh_kv, head_hidden, norm_gain, kv_weight, kv_store, split_blocks, tail_counts, holder_list, slot_list):
    copy_step = RANKS // KVH
    group_size = QH // KVH
    head_rows = HEADB * BLK
    loaded_rows = TCELLS * BLK
    positions = jnp.arange(head_rows, dtype=jnp.int32)
    store_heads = kv_store[:, :, ::copy_step, :]
    fresh_heads = fresh_kv[:, :, ::copy_step, :]
    gain_row = norm_gain.astype(jnp.float32)

    def session(session_id):
        hidden = head_hidden[session_id].astype(jnp.float32)
        scaled = (hidden * gain_row).astype(jnp.bfloat16)
        inverse_rms = lax.rsqrt(lax.optimization_barrier(jnp.sum(hidden * hidden, axis=-1, keepdims=True)) / D + 1e-05)
        projected = jnp.dot(scaled, kv_weight, preferred_element_type=jnp.float32) * inverse_rms
        projected = projected.reshape(head_rows, KVH, 2 * HD)
        head_keys = lax.optimization_barrier(rotate_keys(projected[..., :HD], positions).astype(jnp.bfloat16))
        head_values = lax.optimization_barrier(projected[..., HD:].astype(jnp.bfloat16))
        store_rows = holder_list[session_id] * TCELLS + slot_list[session_id]
        loaded = jnp.take(store_heads, store_rows, axis=0).reshape(loaded_rows, KVH, 2 * HD)
        fresh_part = fresh_heads[session_id]
        key_rows = jnp.concatenate([head_keys, loaded[..., :HD], fresh_part[..., :HD]], axis=0).astype(jnp.float32)
        value_rows = jnp.concatenate([head_values, loaded[..., HD:], fresh_part[..., HD:]], axis=0).astype(jnp.float32)
        head_live = positions < split_blocks[session_id] * BLK
        loaded_live = jnp.arange(loaded_rows, dtype=jnp.int32) // BLK < tail_counts[session_id]
        query_index = jnp.arange(NEW, dtype=jnp.int32)
        fresh_live = query_index[None, :] <= query_index[:, None]
        admitted = jnp.concatenate([jnp.broadcast_to(head_live[None, :], (NEW, head_rows)), jnp.broadcast_to(loaded_live[None, :], (NEW, loaded_rows)), fresh_live], axis=1)
        query_rows = queries[session_id].reshape(NEW, KVH, group_size, HD).astype(jnp.float32)

        def kv_head(head_id):
            query_part = lax.dynamic_index_in_dim(query_rows, head_id, 1, keepdims=False)
            keys_part = lax.dynamic_index_in_dim(key_rows, head_id, 1, keepdims=False)
            values_part = lax.dynamic_index_in_dim(value_rows, head_id, 1, keepdims=False)
            scores = jnp.einsum('ngd,ld->gnl', query_part, keys_part) / math.sqrt(HD)
            scores = jnp.where(admitted[None], scores, -jnp.inf)
            row_peak = lax.optimization_barrier(jnp.max(scores, axis=-1, keepdims=True))
            exp_terms = jnp.exp(scores - row_peak)
            denominator = lax.optimization_barrier(jnp.sum(exp_terms, axis=-1))
            weights = lax.optimization_barrier(exp_terms.astype(jnp.bfloat16))
            mixed = jnp.einsum('gnl,ld->ngd', weights.astype(jnp.float32), values_part)
            return (mixed / jnp.transpose(denominator)[:, :, None]).astype(jnp.bfloat16)
        per_head = lax.map(kv_head, jnp.arange(KVH, dtype=jnp.int32))
        return jnp.transpose(per_head, (1, 0, 2, 3)).reshape(NEW, QH * HD)
    return lax.map(session, jnp.arange(SESSIONS, dtype=jnp.int32))
```

```python
import functools
import math

import jax
import jax.numpy as jnp
from jax import lax
from jax.experimental import pallas as pl
from jax.experimental.pallas import tpu as pltpu
from jax.sharding import Mesh, PartitionSpec as P

F32 = jnp.float32
BF16 = jnp.bfloat16
NT = (((1,), (1,)), ((), ()))
LOW = -1e30
VMEM_LIMIT = 56 * 2**20
QUAD = ("xl", "core")
COMP = ("y", "xl", "core")
POOL = ("xh", "z")


def params():
    return pltpu.CompilerParams(vmem_limit_bytes=VMEM_LIMIT)


def pack_kernel(me_ref, tail_ref, holder_ref, slot_ref, store_ref, out_ref, index_vmem, index_smem, sem, sems):
    sessions, cells = holder_ref.shape
    share = out_ref.shape[1] // store_ref.shape[1]
    rows = store_ref.shape[1]
    row = lax.broadcasted_iota(jnp.int32, (sessions, cells), 0)
    cell = lax.broadcasted_iota(jnp.int32, (sessions, cells), 1)
    tails = jnp.zeros((sessions, cells), jnp.int32)
    for s in range(sessions):
        tails = jnp.where(row == s, tail_ref[s], tails)
    held = (holder_ref[...] == me_ref[0]) & (cell < tails)
    before = lax.broadcasted_iota(jnp.int32, (cells, cells), 0)
    until = lax.broadcasted_iota(jnp.int32, (cells, cells), 1)
    order = jnp.dot(
        jnp.where(held, 1.0, 0.0).astype(BF16),
        jnp.where(before <= until, 1.0, 0.0).astype(BF16),
        preferred_element_type=F32,
    )
    lane = lax.broadcasted_iota(jnp.int32, (sessions, 128), 1)
    packed = jnp.zeros((sessions, 128), jnp.int32)
    for k in range(share):
        wanted = (me_ref[1] * share + k + 1).astype(F32)
        pick = jnp.where(held & (order == wanted), slot_ref[...], 0)
        packed = jnp.where(lane == k, jnp.sum(pick, axis=1, keepdims=True), packed)
    index_vmem[...] = packed
    copy = pltpu.make_async_copy(index_vmem, index_smem, sem)
    copy.start()
    copy.wait()

    def block_copy(s, k):
        return pltpu.make_async_copy(
            store_ref.at[index_smem[s, k]], out_ref.at[s, pl.ds(k * rows, rows)], sems.at[s * share + k]
        )

    for s in range(sessions):
        for k in range(share):
            block_copy(s, k).start()
    for s in range(sessions):
        for k in range(share):
            block_copy(s, k).wait()


def pack_blocks(me, tail_counts, holder_list, slot_list, store, share):
    sessions, cells = holder_list.shape
    _, rows, width = store.shape
    whole = pl.BlockSpec(memory_space=pltpu.VMEM)
    return pl.pallas_call(
        pack_kernel,
        out_shape=jax.ShapeDtypeStruct((sessions, share * rows, width), store.dtype),
        in_specs=[
            pl.BlockSpec(memory_space=pltpu.SMEM),
            pl.BlockSpec(memory_space=pltpu.SMEM),
            whole,
            whole,
            pl.BlockSpec(memory_space=pl.ANY),
        ],
        out_specs=pl.BlockSpec(memory_space=pl.ANY),
        scratch_shapes=[
            pltpu.VMEM((sessions, 128), jnp.int32),
            pltpu.SMEM((sessions, 128), jnp.int32),
            pltpu.SemaphoreType.DMA(()),
            pltpu.SemaphoreType.DMA((sessions * share,)),
        ],
        compiler_params=params(),
        name="pack_blocks",
    )(me, tail_counts, holder_list, slot_list, store)


def project_kernel(hidden_ref, gain_ref, weight_ref, out_ref):
    hidden = hidden_ref[...].astype(F32)
    rows = hidden.shape[0]
    quarter = out_ref.shape[1] - 16
    parts = rows // quarter
    width = out_ref.shape[2]
    scaled = (hidden * gain_ref[...].astype(F32)).astype(BF16)
    squares = lax.dot_general(
        jnp.ones((16, hidden.shape[1]), F32), hidden * hidden, NT,
        precision=lax.Precision.HIGHEST, preferred_element_type=F32,
    )
    high = squares.astype(BF16)
    low = (squares - high.astype(F32)).astype(BF16)
    tail = jnp.concatenate([high, low], axis=1)
    for head in range(weight_ref.shape[1] // width):
        part = jnp.dot(
            scaled, weight_ref[:, head * width : (head + 1) * width], preferred_element_type=F32
        ).astype(BF16)
        for t in range(parts):
            out_ref[head * parts + t, :quarter, :] = part[t * quarter : (t + 1) * quarter]
            out_ref[head * parts + t, quarter:, :] = tail


def project(hidden, gain, weight, heads, parts):
    rows = hidden.shape[0]
    width = weight.shape[1] // heads
    return pl.pallas_call(
        project_kernel,
        out_shape=jax.ShapeDtypeStruct((heads * parts, rows // parts + 16, width), BF16),
        compiler_params=params(),
        name="project",
    )(hidden, gain, weight)


def finish_kernel(width_total, quad_ref, recv_ref, cos_ref, sin_ref, out_ref):
    rows, width = out_ref.shape
    half = width // 2
    total = recv_ref[0].astype(F32)
    for i in range(1, recv_ref.shape[0]):
        total = total + recv_ref[i].astype(F32)
    lane = lax.broadcasted_iota(jnp.int32, (rows, half), 1)
    row = lax.broadcasted_iota(jnp.int32, (rows, half), 0)
    squares = total[rows : rows + 1, :half] + total[rows : rows + 1, half:]
    squares = jnp.sum(
        jnp.where(lane == row + quad_ref[0] * rows, squares, 0.0), axis=1, keepdims=True
    )
    block = total[:rows] * lax.rsqrt(squares / width_total + 1e-05)
    keys = block[:, :half]
    swapped = jnp.concatenate([keys[:, half // 2 :], keys[:, : half // 2]], axis=1)
    out_ref[:, :half] = (keys * cos_ref[...] + swapped * sin_ref[...]).astype(BF16)
    out_ref[:, half:] = block[:, half:].astype(BF16)


def finish(width_total, quad, received, cosine, sine):
    vmem = pl.BlockSpec(memory_space=pltpu.VMEM)
    return pl.pallas_call(
        functools.partial(finish_kernel, width_total),
        out_shape=jax.ShapeDtypeStruct((received.shape[1] - 16, received.shape[2]), BF16),
        in_specs=[pl.BlockSpec(memory_space=pltpu.SMEM), vmem, vmem, vmem],
        out_specs=vmem,
        compiler_params=params(),
        name="finish_head",
    )(quad, received, cosine, sine)


def scaled_queries(queries, head_dim):
    scaled = queries.astype(F32) * (math.log2(math.e) / math.sqrt(head_dim))
    high = scaled.astype(BF16)
    low = (scaled - high.astype(F32)).astype(BF16)
    return jnp.concatenate([high, low], axis=1)


def fresh_kernel(block, queries_ref, fresh_ref, mixed_ref, stats_ref):
    rows, width = queries_ref.shape
    head_dim = fresh_ref.shape[1] // 2
    heads = width // head_dim
    lane = lax.broadcasted_iota(jnp.int32, (block, 128), 1)
    row = lax.broadcasted_iota(jnp.int32, (block, block), 0)
    column = lax.broadcasted_iota(jnp.int32, (block, block), 1)
    for b in range(rows // block):
        here = pl.ds(b * block, block)
        reach = (b + 1) * block
        keys = fresh_ref[:reach, :head_dim]
        keys = jnp.concatenate([keys, keys], axis=1)
        values = fresh_ref[:reach, head_dim:]
        values = jnp.concatenate([values, jnp.ones_like(values)], axis=1)
        stats = jnp.zeros((block, 128), F32)
        for h in range(heads):
            query = scaled_queries(queries_ref[here, h * head_dim : (h + 1) * head_dim], head_dim)
            scores = lax.dot_general(query, keys, NT, preferred_element_type=F32)
            last = jnp.where(column <= row, scores[:, b * block :], LOW)
            if b:
                scores = jnp.concatenate([scores[:, : b * block], last], axis=1)
            else:
                scores = last
            peak = jnp.max(scores, axis=1, keepdims=True)
            terms = jnp.exp2(scores - peak).astype(BF16)
            mixed = jnp.dot(terms, values, preferred_element_type=F32)
            mixed_ref[here, h * head_dim : (h + 1) * head_dim] = mixed[:, :head_dim]
            stats = jnp.where(lane == 2 * h, peak, stats)
            stats = jnp.where(lane == 2 * h + 1, mixed[:, head_dim:], stats)
        stats_ref[here, :] = stats


def attend_fresh(queries, fresh):
    rows, width = queries.shape
    return pl.pallas_call(
        functools.partial(fresh_kernel, min(256, rows)),
        out_shape=(
            jax.ShapeDtypeStruct((rows, width), F32),
            jax.ShapeDtypeStruct((rows, 128), F32),
        ),
        compiler_params=params(),
        cost_estimate=pl.CostEstimate(flops=2 * 2**30, bytes_accessed=2**21, transcendentals=2**20),
        name="attend_fresh",
    )(queries, fresh)


def loaded_kernel(
    chunk, counts_ref, queries_ref, own_ref, other_ref, head_ref, mixed_ref, stats_ref, out_ref, keys_all, values_all
):
    holders, slab, width = own_ref.shape
    head_dim = width // 2
    head_rows = head_ref.shape[0]
    loaded_rows = 2 * holders * slab
    share = 2
    rows = slab // share
    full = counts_ref[holders]
    live_rows = counts_ref[holders + 1]
    core = counts_ref[holders + 2]

    @pl.when(pl.program_id(0) == 0)
    def _():
        def fill(holder, _):
            count = counts_ref[holder]
            for side, ref in enumerate((own_ref, other_ref)):
                for k in range(share):
                    place = jnp.where(core == side, k, share + k)
                    live = place < count
                    source = jnp.where(live, holder, full)
                    block = ref[source, k * rows : (k + 1) * rows, :]
                    weight = jnp.where(live, 1.0, 0.0).astype(BF16)
                    start = pl.multiple_of(side * holders * slab + holder * slab + k * rows, rows)
                    here = pl.ds(start, rows)
                    keys_all[here, :head_dim] = block[:, :head_dim]
                    keys_all[here, head_dim:] = block[:, :head_dim]
                    values_all[here, :head_dim] = block[:, head_dim:] * weight
                    values_all[here, head_dim:] = jnp.full((rows, head_dim), weight, BF16)
            return 0

        lax.fori_loop(0, holders, fill, 0)
        position = lax.broadcasted_iota(jnp.int32, (head_rows, head_dim), 0)
        admitted = position < live_rows
        spare = jnp.broadcast_to(own_ref[full, 0:1, :head_dim].astype(F32), (head_rows, head_dim))
        keys = jnp.where(admitted, head_ref[:, :head_dim].astype(F32), spare).astype(BF16)
        keys_all[loaded_rows:, :head_dim] = keys
        keys_all[loaded_rows:, head_dim:] = keys
        values = jnp.where(admitted, head_ref[:, head_dim:].astype(F32), 0.0).astype(BF16)
        values_all[loaded_rows:, :head_dim] = values
        values_all[loaded_rows:, head_dim:] = jnp.where(admitted, 1.0, 0.0).astype(BF16)

    heads = queries_ref.shape[1] // head_dim
    query = [
        scaled_queries(queries_ref[:, h * head_dim : (h + 1) * head_dim], head_dim) for h in range(heads)
    ]
    peak = [stats_ref[:, 2 * h : 2 * h + 1] for h in range(heads)]
    mixed = [
        jnp.concatenate(
            [
                mixed_ref[:, h * head_dim : (h + 1) * head_dim],
                jnp.broadcast_to(stats_ref[:, 2 * h + 1 : 2 * h + 2], (queries_ref.shape[0], head_dim)),
            ],
            axis=1,
        )
        for h in range(heads)
    ]
    starts = list(range(0, loaded_rows, chunk))
    for start in starts:
        stop = start + chunk if start != starts[-1] else loaded_rows + head_rows
        for h in range(heads):
            scores = lax.dot_general(query[h], keys_all[start:stop, :], NT, preferred_element_type=F32)
            higher = jnp.maximum(peak[h], jnp.max(scores, axis=1, keepdims=True))
            terms = jnp.exp2(scores - higher).astype(BF16)
            mixed[h] = mixed[h] * jnp.exp2(peak[h] - higher) + jnp.dot(
                terms, values_all[start:stop, :], preferred_element_type=F32
            )
            peak[h] = higher
    for h in range(heads):
        out_ref[:, h * head_dim : (h + 1) * head_dim] = (
            mixed[h][:, :head_dim] / mixed[h][:, head_dim:]
        ).astype(BF16)


def attend_loaded(counts, queries, own, other, head, mixed, stats):
    rows, width = queries.shape
    block = min(512, rows)
    total = own.shape[0] * own.shape[1] * 2 + head.shape[0]
    whole = lambda shape: pl.BlockSpec(shape, lambda i, counts: (0,) * len(shape))
    rowed = lambda columns: pl.BlockSpec((block, columns), lambda i, counts: (i, 0))
    return pl.pallas_call(
        functools.partial(loaded_kernel, 512),
        grid_spec=pltpu.PrefetchScalarGridSpec(
            num_scalar_prefetch=1,
            grid=(rows // block,),
            in_specs=[
                rowed(width),
                whole(own.shape),
                whole(other.shape),
                whole(head.shape),
                rowed(width),
                rowed(128),
            ],
            out_specs=rowed(width),
            scratch_shapes=[pltpu.VMEM((total, 256), BF16), pltpu.VMEM((total, 256), BF16)],
        ),
        out_shape=jax.ShapeDtypeStruct((rows, width), BF16),
        compiler_params=params(),
        name="attend_loaded",
    )(counts, queries, own, other, head, mixed, stats)


def per_device(
    queries,
    fresh_kv,
    head_hidden,
    norm_gain,
    kv_weight,
    kv_store,
    split_blocks,
    tail_counts,
    holder_list,
    slot_list,
):
    pool_rank = lax.axis_index(POOL)
    core = lax.axis_index("core")
    quad = lax.axis_index(QUAD)
    quads = lax.axis_size(QUAD)
    holders = lax.axis_size(POOL)
    heads = lax.axis_size("y")
    ranks = lax.axis_size(COMP)
    cells = holder_list.shape[1]
    capacity = cells // holders
    block_rows = kv_store.shape[1]
    head_dim = kv_store.shape[3] // 2
    head_rows = head_hidden.shape[1]

    store = kv_store[:, :, 0, :]
    me = jnp.stack([pool_rank, core]).astype(jnp.int32)
    outgoing = pack_blocks(me, tail_counts, holder_list, slot_list, store, capacity // 2)
    own = lax.all_to_all(outgoing, POOL, split_axis=0, concat_axis=0, tiled=True)

    partial_sums = project(head_hidden[0], norm_gain[None, :], kv_weight, heads, quads)
    partial_sums = lax.all_to_all(partial_sums, COMP, split_axis=0, concat_axis=0, tiled=True)

    mixed, stats = attend_fresh(queries[0], fresh_kv[0, :, 0, :])

    quarter = head_rows // quads
    positions = (quad * quarter + jnp.arange(quarter, dtype=jnp.int32)).astype(F32)
    frequency = 500000.0 ** (-2.0 * jnp.arange(head_dim // 2, dtype=F32) / head_dim)
    angles = positions[:, None] * frequency[None, :]
    cosine = jnp.cos(angles)
    sine = jnp.sin(angles)
    cosine = jnp.concatenate([cosine, cosine], axis=1)
    sine = jnp.concatenate([-sine, sine], axis=1)
    head = finish(
        head_hidden.shape[2] * ranks, quad.astype(jnp.int32)[None], partial_sums, cosine, sine
    )
    head = lax.all_gather(head, QUAD, axis=0, tiled=True)

    own_holders = lax.dynamic_index_in_dim(holder_list, pool_rank, 0, keepdims=False)
    own_ok = jnp.arange(cells, dtype=jnp.int32) < lax.dynamic_index_in_dim(
        tail_counts, pool_rank, 0, keepdims=False
    )
    holder_ids = jnp.arange(holders, dtype=jnp.int32)
    counts = jnp.sum(
        ((own_holders[None, :] == holder_ids[:, None]) & own_ok[None, :]).astype(jnp.int32), axis=1
    )
    counts = jnp.concatenate(
        [
            counts,
            jnp.argmax(counts).astype(jnp.int32)[None],
            split_blocks * block_rows,
            core.astype(jnp.int32)[None],
        ]
    )
    other = lax.ppermute(own, "core", [(0, 1), (1, 0)])
    return attend_loaded(counts, queries[0], own, other, head, mixed, stats)[None]


def solution(mesh):
    fine = Mesh(mesh.devices.reshape(2, 8, 8, 2, 2), ("xh", "z", "y", "xl", "core"))
    return jax.shard_map(
        per_device,
        mesh=fine,
        in_specs=(
            P(POOL, None, COMP),
            P(POOL, None, COMP, None),
            P(POOL, None, COMP),
            P(COMP),
            P(COMP, None),
            P(POOL, None, COMP, None),
            P(POOL),
            P(),
            P(),
            P(),
        ),
        out_specs=P(POOL, None, COMP),
        check_vma=False,
    )
```

```python
import functools
import math

import jax
import jax.numpy as jnp
from jax import lax
from jax.experimental import pallas as pl
from jax.experimental.pallas import tpu as pltpu
from jax.sharding import Mesh, PartitionSpec as P

F32 = jnp.float32
BF16 = jnp.bfloat16
NT = (((1,), (1,)), ((), ()))
LOW = -1e30
VMEM_LIMIT = 56 * 2**20
QUAD = ("xl", "core")
COMP = ("y", "xl", "core")
POOL = ("xh", "z")
SWAP = [(0, 1), (1, 0)]
SMEM = pl.BlockSpec(memory_space=pltpu.SMEM)
VMEM = pl.BlockSpec(memory_space=pltpu.VMEM)


def params():
    return pltpu.CompilerParams(vmem_limit_bytes=VMEM_LIMIT)


def pack_kernel(tail_ref, holder_ref, slot_ref, store_ref, out_ref, index_vmem, index_smem, staged, sem, in_sems, out_sems):
    sessions, cells = holder_ref.shape
    rows = store_ref.shape[1]
    share = out_ref.shape[1] // rows
    me = lax.axis_index("xh") * lax.axis_size("z") + lax.axis_index("z")
    core = lax.axis_index("core")
    row = lax.broadcasted_iota(jnp.int32, (sessions, cells), 0)
    cell = lax.broadcasted_iota(jnp.int32, (sessions, cells), 1)
    tails = jnp.zeros((sessions, cells), jnp.int32)
    for s in range(sessions):
        tails = jnp.where(row == s, tail_ref[s], tails)
    held = (holder_ref[...] == me) & (cell < tails)
    before = lax.broadcasted_iota(jnp.int32, (cells, cells), 0)
    until = lax.broadcasted_iota(jnp.int32, (cells, cells), 1)
    order = jnp.dot(
        jnp.where(held, 1.0, 0.0).astype(BF16),
        jnp.where(before <= until, 1.0, 0.0).astype(BF16),
        preferred_element_type=F32,
    )
    lane = lax.broadcasted_iota(jnp.int32, (sessions, 128), 1)
    packed = jnp.zeros((sessions, 128), jnp.int32)
    for k in range(share):
        wanted = (core * share + k + 1).astype(F32)
        pick = jnp.where(held & (order == wanted), slot_ref[...], 0)
        packed = jnp.where(lane == k, jnp.sum(pick, axis=1, keepdims=True), packed)
    index_vmem[...] = packed
    copy = pltpu.make_async_copy(index_vmem, index_smem, sem)
    copy.start()
    copy.wait()

    def block_in(s, k):
        return pltpu.make_async_copy(
            store_ref.at[index_smem[s, k]], staged.at[s, pl.ds(k * rows, rows)], in_sems.at[s * share + k]
        )

    def slab_out(s):
        return pltpu.make_async_copy(staged.at[s], out_ref.at[s], out_sems.at[s])

    for s in range(sessions):
        for k in range(share):
            block_in(s, k).start()
    for s in range(sessions):
        for k in range(share):
            block_in(s, k).wait()
        slab_out(s).start()
    for s in range(sessions):
        slab_out(s).wait()


def pack_blocks(tail_counts, holder_list, slot_list, store, share):
    sessions, cells = holder_list.shape
    _, rows, width = store.shape
    return pl.pallas_call(
        pack_kernel,
        out_shape=jax.ShapeDtypeStruct((sessions, share * rows, width), store.dtype),
        in_specs=[SMEM, VMEM, VMEM, pl.BlockSpec(memory_space=pl.ANY)],
        out_specs=pl.BlockSpec(memory_space=pl.ANY),
        scratch_shapes=[
            pltpu.VMEM((sessions, 128), jnp.int32),
            pltpu.SMEM((sessions, 128), jnp.int32),
            pltpu.VMEM((sessions, share * rows, width), store.dtype),
            pltpu.SemaphoreType.DMA(()),
            pltpu.SemaphoreType.DMA((sessions * share,)),
            pltpu.SemaphoreType.DMA((sessions,)),
        ],
        compiler_params=params(),
        name="pack_blocks",
    )(tail_counts, holder_list, slot_list, store)


EXTRA = 16


def split_squares(total, rows):
    half = total.shape[1] // 2
    return total[:rows], total[rows:, :half] + total[rows:, half:]


def in_bfloat16(total, rows):
    main, squares = split_squares(total, rows)
    high = squares.astype(BF16)
    low = (squares - high.astype(F32)).astype(BF16)
    return jnp.concatenate([main.astype(BF16), jnp.concatenate([high, low], axis=1)], axis=0)


def block_counts(tail_ref, holder_ref, counts_ref):
    cells = holder_ref.shape[1]
    holders = counts_ref.shape[0]
    session = lax.axis_index("xh") * lax.axis_size("z") + lax.axis_index("z")
    holder = lax.broadcasted_iota(jnp.int32, (holders, cells), 0)
    cell = lax.broadcasted_iota(jnp.int32, (holders, cells), 1)
    match = (holder_ref[pl.ds(session, 1), :] == holder) & (cell < tail_ref[session])
    found = jnp.sum(jnp.where(match, 1.0, 0.0), axis=1, keepdims=True).astype(jnp.int32)
    ids = lax.broadcasted_iota(jnp.int32, (holders, 1), 0)
    full = jnp.max(jnp.where(found >= cells // holders, ids, 0).astype(F32), axis=0, keepdims=True)
    lane = lax.broadcasted_iota(jnp.int32, counts_ref.shape, 1)
    counts = jnp.where(lane == 0, found, 0)
    counts = jnp.where(lane == 1, full.astype(jnp.int32), counts)
    counts_ref[...] = jnp.where(lane == 2, lax.axis_index("core"), counts)


def project_kernel(tail_ref, holder_ref, hidden_ref, gain_ref, weight_ref, send_ref, keep_ref, counts_ref):
    hidden = hidden_ref[...].astype(F32)
    rows = hidden.shape[0]
    width = send_ref.shape[2]
    core = lax.axis_index("core")
    scaled = (hidden * gain_ref[...].astype(F32)).astype(BF16)
    squares = lax.dot_general(
        jnp.ones((EXTRA, hidden.shape[1]), F32), hidden * hidden, NT,
        precision=lax.Precision.HIGHEST, preferred_element_type=F32,
    )
    tail = jnp.concatenate([squares, jnp.zeros_like(squares)], axis=1)
    for out_ref, side in ((send_ref, 1 - core), (keep_ref, core)):
        for x in range(2):
            for j in range(2):
                start = pl.multiple_of((4 * x + 2 * side + j) * width, width)
                out_ref[2 * x + j, :rows, :] = jnp.dot(
                    scaled, weight_ref[:, pl.ds(start, width)], preferred_element_type=F32
                )
                out_ref[2 * x + j, rows:, :] = tail
    block_counts(tail_ref, holder_ref, counts_ref)


def project(tail_counts, holder_list, hidden, gain, weight, heads, holders):
    rows = hidden.shape[0]
    out = jax.ShapeDtypeStruct((heads // 2, rows + EXTRA, weight.shape[1] // heads), F32)
    return pl.pallas_call(
        project_kernel,
        out_shape=(out, out, jax.ShapeDtypeStruct((holders, 128), jnp.int32)),
        in_specs=[SMEM, VMEM, VMEM, VMEM, VMEM],
        compiler_params=params(),
        name="project",
    )(tail_counts, holder_list, hidden, gain, weight)


def join_cores_kernel(recv_ref, mine_ref, *out_refs):
    rows = recv_ref.shape[1] - EXTRA
    turn = lax.rem(lax.axis_index("y"), 4)
    for t, out_ref in enumerate(out_refs):
        head = t ^ turn
        out_ref[...] = in_bfloat16(recv_ref[head] + mine_ref[head], rows)


def join_cores(received, mine):
    out = jax.ShapeDtypeStruct(received.shape[1:], BF16)
    return pl.pallas_call(
        join_cores_kernel, out_shape=(out,) * received.shape[0], compiler_params=params(), name="join_cores"
    )(received, mine)


def join_chips_kernel(*refs):
    total = refs[0][...].astype(F32)
    for ref in refs[1:-1]:
        total = total + ref[...].astype(F32)
    refs[-1][...] = in_bfloat16(total, total.shape[0] - EXTRA)


def join_chips(arrived):
    return pl.pallas_call(
        join_chips_kernel,
        out_shape=jax.ShapeDtypeStruct(arrived[0].shape, BF16),
        compiler_params=params(),
        name="join_chips",
    )(*arrived)


def owners_of_turn(turn):
    pairs = []
    for y in range(8):
        for xl in range(2):
            for core in range(2):
                head = turn ^ (y % 4)
                owner = 4 * (head // 2) + 2 * core + head % 2
                pairs.append((y * 4 + xl * 2 + core, owner * 4 + xl * 2 + y // 4))
    return pairs


def head_sums(tail_counts, holder_list, hidden, gain, weight, heads, holders):
    send, keep, counts = project(tail_counts, holder_list, hidden, gain, weight, heads, holders)
    turns = join_cores(lax.ppermute(send, "core", SWAP), keep)
    arrived = [lax.ppermute(turn, COMP, owners_of_turn(t)) for t, turn in enumerate(turns)]
    return counts, arrived


def rotation(rows, head_dim):
    positions = jnp.arange(rows, dtype=jnp.int32).astype(F32)
    frequency = 500000.0 ** (-2.0 * jnp.arange(head_dim // 2, dtype=F32) / head_dim)
    angles = positions[:, None] * frequency[None, :]
    cosine = jnp.cos(angles)
    sine = jnp.sin(angles)
    return jnp.concatenate([cosine, cosine], axis=1), jnp.concatenate([-sine, sine], axis=1)


def finish_head(width_total, gathered_ref, cos_ref, sin_ref):
    rows = gathered_ref.shape[1] - EXTRA
    half = gathered_ref.shape[2] // 2
    total = gathered_ref[0].astype(F32)
    for i in range(1, gathered_ref.shape[0]):
        total = total + gathered_ref[i].astype(F32)
    main, squares = split_squares(total, rows)
    lane = lax.broadcasted_iota(jnp.int32, (rows, half), 1)
    row = lax.broadcasted_iota(jnp.int32, (rows, half), 0)
    squares = jnp.sum(jnp.where(lane == row, squares[:1], 0.0), axis=1, keepdims=True)
    block = main * lax.rsqrt(squares / width_total + 1e-05)
    keys = block[:, :half]
    swapped = jnp.concatenate([keys[:, half // 2 :], keys[:, : half // 2]], axis=1)
    return keys * cos_ref[...] + swapped * sin_ref[...], block[:, half:]


def scaled_queries(queries, head_dim):
    scaled = queries.astype(F32) * (math.log2(math.e) / math.sqrt(head_dim))
    high = scaled.astype(BF16)
    low = (scaled - high.astype(F32)).astype(BF16)
    return jnp.concatenate([high, low], axis=1)


def extend(state, query, keys, values, mask=None):
    scores = lax.dot_general(query, keys, NT, preferred_element_type=F32)
    if mask is not None:
        scores = jnp.where(mask, scores, LOW)
    peak = jnp.max(scores, axis=1, keepdims=True)
    if state is not None:
        peak = jnp.maximum(peak, state[0])
    mixed = jnp.dot(jnp.exp2(scores - peak).astype(BF16), values, preferred_element_type=F32)
    if state is not None:
        mixed = mixed + state[1] * jnp.exp2(state[0] - peak)
    return peak, mixed


def attend_kernel(block, chunk, width_total, counts_ref, split_ref, queries_ref, fresh_ref, own_ref, other_ref,
                  gathered_ref, cos_ref, sin_ref, out_ref, blocks, live, sems):
    holders, slab, width = own_ref.shape
    head_dim = width // 2
    head_rows = gathered_ref.shape[1] - EXTRA
    loaded_rows = 2 * holders * slab
    share = 2
    rows = slab // share
    full = counts_ref[0, 1]
    core = counts_ref[0, 2]
    copies = [
        pltpu.make_async_copy(ref, blocks.at[pl.ds(side * holders, holders)], sems.at[side])
        for side, ref in enumerate((own_ref, other_ref))
    ]
    for copy in copies:
        copy.start()
    live[...] = jnp.ones(live.shape, BF16)

    def gather_blocks():
        for copy in copies:
            copy.wait()

        def mend(holder, _):
            for side in range(2):
                for k in range(share):

                    @pl.when((core if side == 0 else 1 - core) * share + k >= counts_ref[holder, 0])
                    def _():
                        here = pl.ds(k * rows, rows)
                        place = side * holders + holder
                        spare = side * holders + full
                        blocks[place, here, :head_dim] = blocks[spare, here, :head_dim]
                        blocks[place, here, head_dim:] = jnp.zeros((rows, head_dim), BF16)
                        live[place, here, :] = jnp.zeros((rows, head_dim), BF16)

            return 0

        lax.fori_loop(0, holders, mend, 0)
        position = lax.broadcasted_iota(jnp.int32, (head_rows, head_dim), 0)
        admitted = position < split_ref[0] * rows
        keys, values = finish_head(width_total, gathered_ref, cos_ref, sin_ref)
        spare = blocks[full, :16, :head_dim].astype(F32)[:1]
        blocks[2 * holders, :head_rows, :head_dim] = jnp.where(admitted, keys, spare).astype(BF16)
        blocks[2 * holders, :head_rows, head_dim:] = jnp.where(admitted, values, 0.0).astype(BF16)
        live[2 * holders, :head_rows, :] = jnp.where(admitted, 1.0, 0.0).astype(BF16)

    heads = queries_ref.shape[1] // head_dim
    total_rows = queries_ref.shape[0]
    row = lax.broadcasted_iota(jnp.int32, (block, block), 0)
    column = lax.broadcasted_iota(jnp.int32, (block, block), 1)
    step = chunk // slab
    starts = list(range(0, 2 * holders, step))

    def doubled(keys):
        return jnp.concatenate([keys, keys], axis=1)

    for b in range(total_rows // block):
        here = pl.ds(b * block, block)
        query = [
            scaled_queries(queries_ref[here, h * head_dim : (h + 1) * head_dim], head_dim) for h in range(heads)
        ]
        state = [None] * heads
        for earlier in range(b + 1):
            there = pl.ds(earlier * block, block)
            keys = doubled(fresh_ref[there, :head_dim])
            values = fresh_ref[there, head_dim:]
            values = jnp.concatenate([values, jnp.ones_like(values)], axis=1)
            for h in range(heads):
                mask = column <= row if earlier == b else None
                state[h] = extend(state[h], query[h], keys, values, mask)
        if b == 0:
            gather_blocks()
        for start in starts:
            parts = list(range(start, start + step))
            taken = [blocks[i] for i in parts]
            weights = [live[i] for i in parts]
            if start == starts[-1]:
                taken.append(blocks[2 * holders, :head_rows])
                weights.append(live[2 * holders, :head_rows])
            taken = jnp.concatenate(taken, axis=0)
            values = jnp.concatenate([taken[:, head_dim:], jnp.concatenate(weights, axis=0)], axis=1)
            for h in range(heads):
                state[h] = extend(state[h], query[h], doubled(taken[:, :head_dim]), values)
        for h in range(heads):
            mixed = state[h][1]
            out_ref[here, h * head_dim : (h + 1) * head_dim] = (
                mixed[:, :head_dim] / mixed[:, head_dim:]
            ).astype(BF16)


def attend(counts, split, queries, fresh, own, other, gathered, width_total):
    rows, width = queries.shape
    holders, slab, pair = own.shape
    cosine, sine = rotation(gathered.shape[1] - EXTRA, pair // 2)
    anywhere = pl.BlockSpec(memory_space=pl.ANY)
    return pl.pallas_call(
        functools.partial(attend_kernel, min(512, rows), 512, width_total),
        in_specs=[SMEM, SMEM, VMEM, VMEM, anywhere, anywhere, VMEM, VMEM, VMEM],
        out_specs=VMEM,
        scratch_shapes=[
            pltpu.VMEM((2 * holders + 1, slab, pair), BF16),
            pltpu.VMEM((2 * holders + 1, slab, pair // 2), BF16),
            pltpu.SemaphoreType.DMA((2,)),
        ],
        out_shape=jax.ShapeDtypeStruct((rows, width), BF16),
        compiler_params=params(),
        cost_estimate=pl.CostEstimate(flops=2**34, bytes_accessed=2**22, transcendentals=2**23),
        name="attend",
    )(counts, split, queries, fresh, own, other, gathered, cosine, sine)


def per_device(
    queries,
    fresh_kv,
    head_hidden,
    norm_gain,
    kv_weight,
    kv_store,
    split_blocks,
    tail_counts,
    holder_list,
    slot_list,
):
    holders = lax.axis_size(POOL)
    capacity = holder_list.shape[1] // holders
    outgoing = pack_blocks(tail_counts, holder_list, slot_list, kv_store[:, :, 0, :], capacity // 2)
    own = lax.all_to_all(outgoing, POOL, split_axis=0, concat_axis=0, tiled=True)
    counts, arrived = head_sums(
        tail_counts, holder_list, head_hidden[0], norm_gain[None, :], kv_weight, lax.axis_size("y"), holders
    )
    own, arrived = lax.optimization_barrier((own, arrived))
    other = lax.ppermute(own, "core", SWAP)
    gathered = lax.all_gather(join_chips(arrived), QUAD, axis=0)
    return attend(
        counts,
        split_blocks,
        queries[0],
        fresh_kv[0, :, 0, :],
        own,
        other,
        gathered,
        head_hidden.shape[2] * lax.axis_size(COMP),
    )[None]


def solution(mesh):
    fine = Mesh(mesh.devices.reshape(2, 8, 8, 2, 2), ("xh", "z", "y", "xl", "core"))
    return jax.shard_map(
        per_device,
        mesh=fine,
        in_specs=(
            P(POOL, None, COMP),
            P(POOL, None, COMP, None),
            P(POOL, None, COMP),
            P(COMP),
            P(COMP, None),
            P(POOL, None, COMP, None),
            P(POOL),
            P(),
            P(),
            P(),
        ),
        out_specs=P(POOL, None, COMP),
        check_vma=False,
    )
```

```python
import functools
import math

import jax
import jax.numpy as jnp
import numpy as np
from jax import lax
from jax.experimental import pallas as pl
from jax.experimental.pallas import tpu as pltpu
from jax.sharding import Mesh, PartitionSpec as P

F32 = jnp.float32
BF16 = jnp.bfloat16
NT = (((1,), (1,)), ((), ()))
LOW = -1e30
QUAD = ("xl", "core")
COMP = ("y", "xl", "core")
POOL = ("xh", "z")
SWAP = [(0, 1), (1, 0)]
SMEM = pl.BlockSpec(memory_space=pltpu.SMEM)
VMEM = pl.BlockSpec(memory_space=pltpu.VMEM)


def params(mebibytes):
    return pltpu.CompilerParams(vmem_limit_bytes=mebibytes * 2**20)


EXTRA = 16


def split_squares(total, rows):
    half = total.shape[1] // 2
    return total[:rows], total[rows:, :half] + total[rows:, half:]


def in_bfloat16(total, rows):
    main, squares = split_squares(total, rows)
    high = squares.astype(BF16)
    low = (squares - high.astype(F32)).astype(BF16)
    return jnp.concatenate([main.astype(BF16), jnp.concatenate([high, low], axis=1)], axis=0)


def block_counts(tail_ref, holder_ref, counts_ref):
    cells = holder_ref.shape[1]
    holders = counts_ref.shape[0]
    session = lax.axis_index("xh") * lax.axis_size("z") + lax.axis_index("z")
    holder = lax.broadcasted_iota(jnp.int32, (holders, cells), 0)
    cell = lax.broadcasted_iota(jnp.int32, (holders, cells), 1)
    match = (holder_ref[pl.ds(session, 1), :] == holder) & (cell < tail_ref[session])
    found = jnp.sum(jnp.where(match, 1.0, 0.0), axis=1, keepdims=True).astype(jnp.int32)
    ids = lax.broadcasted_iota(jnp.int32, (holders, 1), 0)
    full = jnp.max(jnp.where(found >= cells // holders, ids, 0).astype(F32), axis=0, keepdims=True)
    lane = lax.broadcasted_iota(jnp.int32, counts_ref.shape, 1)
    counts = jnp.where(lane == 0, found, 0)
    counts = jnp.where(lane == 1, full.astype(jnp.int32), counts)
    counts_ref[...] = jnp.where(lane == 2, lax.axis_index("core"), counts)


def offsets(turn):
    return 3 - turn, turn - 4


def held_slots(share, tail_ref, holder_ref, slot_ref):
    sessions, cells = holder_ref.shape
    me = lax.axis_index("xh") * lax.axis_size("z") + lax.axis_index("z")
    core = lax.axis_index("core")
    row = lax.broadcasted_iota(jnp.int32, (sessions, cells), 0)
    cell = lax.broadcasted_iota(jnp.int32, (sessions, cells), 1)
    tails = jnp.zeros((sessions, cells), jnp.int32)
    for s in range(sessions):
        tails = jnp.where(row == s, tail_ref[s], tails)
    held = (holder_ref[...] == me) & (cell < tails)
    before = lax.broadcasted_iota(jnp.int32, (cells, cells), 0)
    until = lax.broadcasted_iota(jnp.int32, (cells, cells), 1)
    order = jnp.dot(
        jnp.where(held, 1.0, 0.0).astype(BF16),
        jnp.where(before <= until, 1.0, 0.0).astype(BF16),
        preferred_element_type=F32,
    )
    lane = lax.broadcasted_iota(jnp.int32, (sessions, 128), 1)
    slots = jnp.zeros((sessions, 128), jnp.int32)
    for k in range(share):
        wanted = (core * share + k + 1).astype(F32)
        pick = jnp.where(held & (order == wanted), slot_ref[...], 0)
        slots = jnp.where(lane == k, jnp.sum(pick, axis=1, keepdims=True), slots)
    return slots


def prepare_kernel(tail_ref, holder_ref, slot_ref, hidden_ref, gain_ref, weight_hbm, store_ref,
                   packed_ref, send_ref, keep_ref, counts_ref,
                   index_vmem, index_smem, staged, weight_ref, send, keep, sems, in_sems, out_sems):
    sessions = holder_ref.shape[0]
    block_rows = store_ref.shape[1]
    share = packed_ref.shape[1] // block_rows
    weight_copy = pltpu.make_async_copy(weight_hbm, weight_ref, sems.at[0])
    weight_copy.start()
    index_vmem[...] = held_slots(share, tail_ref, holder_ref, slot_ref)
    index_copy = pltpu.make_async_copy(index_vmem, index_smem, sems.at[1])
    index_copy.start()
    index_copy.wait()

    def block_in(s, k):
        return pltpu.make_async_copy(
            store_ref.at[index_smem[s, k]],
            staged.at[s, pl.ds(k * block_rows, block_rows)],
            in_sems.at[s * share + k],
        )

    def slab_out(s):
        return pltpu.make_async_copy(staged.at[s], packed_ref.at[s], out_sems.at[s])

    for s in range(sessions):
        for k in range(share):
            block_in(s, k).start()

    hidden = hidden_ref[...].astype(F32)
    rows = hidden.shape[0]
    width = send.shape[2]
    core = lax.axis_index("core")
    scaled = (hidden * gain_ref[...].astype(F32)[None, :]).astype(BF16)
    squares = lax.dot_general(
        jnp.ones((EXTRA, hidden.shape[1]), F32), hidden * hidden, NT,
        precision=lax.Precision.HIGHEST, preferred_element_type=F32,
    )
    weight_copy.wait()

    def partial_sums(t, side):
        head = lax.rem(lax.axis_index("y") + jnp.where(side == 0, *offsets(t)) + 8, 8)
        columns = pl.ds(pl.multiple_of(head * width, width), width)
        return jnp.dot(scaled, weight_ref[:, columns], preferred_element_type=F32)

    high = squares.astype(BF16)
    low = (squares - high.astype(F32)).astype(BF16)
    for t in range(4):
        send[t, :rows, :] = partial_sums(t, 1 - core).astype(BF16)
        send[t, rows:, :] = jnp.concatenate([high, low], axis=1)
    send_copy = pltpu.make_async_copy(send, send_ref, sems.at[2])
    send_copy.start()
    for t in range(4):
        keep[t, :rows, :] = partial_sums(t, core)
        keep[t, rows:, :] = jnp.concatenate([squares, jnp.zeros_like(squares)], axis=1)
    keep_copy = pltpu.make_async_copy(keep, keep_ref, sems.at[3])
    keep_copy.start()
    block_counts(tail_ref, holder_ref, counts_ref)

    for s in range(sessions):
        for k in range(share):
            block_in(s, k).wait()
        slab_out(s).start()
    send_copy.wait()
    keep_copy.wait()
    for s in range(sessions):
        slab_out(s).wait()


def prepare(tail_counts, holder_list, slot_list, hidden, gain, weight, store, share, holders, heads):
    sessions, cells = holder_list.shape
    _, block_rows, width = store.shape
    partials = (heads // 2, hidden.shape[0] + EXTRA, width)
    packed = (sessions, share * block_rows, width)
    anywhere = pl.BlockSpec(memory_space=pl.ANY)
    return pl.pallas_call(
        prepare_kernel,
        out_shape=(
            jax.ShapeDtypeStruct(packed, BF16),
            jax.ShapeDtypeStruct(partials, BF16),
            jax.ShapeDtypeStruct(partials, F32),
            jax.ShapeDtypeStruct((holders, 128), jnp.int32),
        ),
        in_specs=[SMEM, VMEM, VMEM, VMEM, VMEM, anywhere, anywhere],
        out_specs=(anywhere, anywhere, anywhere, VMEM),
        scratch_shapes=[
            pltpu.VMEM((sessions, 128), jnp.int32),
            pltpu.SMEM((sessions, 128), jnp.int32),
            pltpu.VMEM(packed, BF16),
            pltpu.VMEM(weight.shape, BF16),
            pltpu.VMEM(partials, BF16),
            pltpu.VMEM(partials, F32),
            pltpu.SemaphoreType.DMA((4,)),
            pltpu.SemaphoreType.DMA((sessions * share,)),
            pltpu.SemaphoreType.DMA((sessions,)),
        ],
        compiler_params=params(56),
        name="prepare",
    )(tail_counts, holder_list, slot_list, hidden, gain, weight, store)


def join_cores_kernel(sent_ref, mine_ref, *out_refs):
    rows = mine_ref.shape[1] - EXTRA
    there = 1 - lax.axis_index("core")
    for t, out_ref in enumerate(out_refs):
        out_ref[...] = in_bfloat16(sent_ref[there, t].astype(F32) + mine_ref[t], rows)


def join_cores(sent, mine):
    out = jax.ShapeDtypeStruct(mine.shape[1:], BF16)
    return pl.pallas_call(
        join_cores_kernel, out_shape=(out,) * mine.shape[0], compiler_params=params(6), name="join_cores"
    )(sent, mine)


def join_chips_kernel(*refs):
    total = refs[0][...].astype(F32)
    for ref in refs[1:-1]:
        total = total + ref[...].astype(F32)
    refs[-1][...] = in_bfloat16(total, total.shape[0] - EXTRA)


def join_chips(arrived):
    return pl.pallas_call(
        join_chips_kernel,
        out_shape=jax.ShapeDtypeStruct(arrived[0].shape, BF16),
        compiler_params=params(6),
        name="join_chips",
    )(*arrived)


def owners_of_turn(turn):
    return [
        (y * 4 + 2 * xl + core, (y + offsets(turn)[core]) % 8 * 4 + 2 * xl + core)
        for y in range(8)
        for xl in range(2)
        for core in range(2)
    ]


def rotation(rows, head_dim):
    frequency = 500000.0 ** (-2.0 * np.arange(head_dim // 2) / head_dim)
    angles = np.arange(rows)[:, None] * frequency[None, :]
    cosine, sine = np.cos(angles), np.sin(angles)
    return (
        jnp.asarray(np.concatenate([cosine, cosine], axis=1), F32),
        jnp.asarray(np.concatenate([-sine, sine], axis=1), F32),
    )


def finish_head(width_total, gathered_ref, cos_ref, sin_ref):
    rows = gathered_ref.shape[1] - EXTRA
    half = gathered_ref.shape[2] // 2
    total = gathered_ref[0].astype(F32)
    for i in range(1, gathered_ref.shape[0]):
        total = total + gathered_ref[i].astype(F32)
    main, squares = split_squares(total, rows)
    lane = lax.broadcasted_iota(jnp.int32, (rows, half), 1)
    row = lax.broadcasted_iota(jnp.int32, (rows, half), 0)
    squares = jnp.sum(jnp.where(lane == row, squares[:1], 0.0), axis=1, keepdims=True)
    block = main * lax.rsqrt(squares / width_total + 1e-05)
    keys = block[:, :half]
    swapped = jnp.concatenate([keys[:, half // 2 :], keys[:, : half // 2]], axis=1)
    return keys * cos_ref[...] + swapped * sin_ref[...], block[:, half:]


def scaled_queries(queries, head_dim):
    scaled = queries.astype(F32) * (math.log2(math.e) / math.sqrt(head_dim))
    high = scaled.astype(BF16)
    low = (scaled - high.astype(F32)).astype(BF16)
    return jnp.concatenate([high, low], axis=1)


def extend(state, query, keys, values, mask=None):
    scores = lax.dot_general(query, keys, NT, preferred_element_type=F32)
    if mask is not None:
        scores = jnp.where(mask, scores, LOW)
    peak = jnp.max(scores, axis=1, keepdims=True)
    if state is not None:
        peak = jnp.maximum(peak, state[0])
    mixed = jnp.dot(jnp.exp2(scores - peak).astype(BF16), values, preferred_element_type=F32)
    if state is not None:
        mixed = mixed + state[1] * jnp.exp2(state[0] - peak)
    return peak, mixed


def attend_kernel(block, chunk, width_total, counts_ref, split_ref, queries_ref, fresh_ref, own_ref, other_ref,
                  gathered_ref, cos_ref, sin_ref, out_ref, blocks, live, sems):
    holders, slab, width = own_ref.shape
    head_dim = width // 2
    head_rows = gathered_ref.shape[1] - EXTRA
    loaded_rows = 2 * holders * slab
    share = 2
    rows = slab // share
    full = counts_ref[0, 1]
    core = counts_ref[0, 2]
    copies = [
        pltpu.make_async_copy(ref, blocks.at[pl.ds(side * holders, holders)], sems.at[side])
        for side, ref in enumerate((own_ref, other_ref))
    ]
    for copy in copies:
        copy.start()
    live[...] = jnp.ones(live.shape, BF16)

    def gather_blocks():
        for copy in copies:
            copy.wait()

        def mend(holder, _):
            for side in range(2):
                for k in range(share):

                    @pl.when((core if side == 0 else 1 - core) * share + k >= counts_ref[holder, 0])
                    def _():
                        here = pl.ds(k * rows, rows)
                        place = side * holders + holder
                        spare = side * holders + full
                        blocks[place, here, :head_dim] = blocks[spare, here, :head_dim]
                        blocks[place, here, head_dim:] = jnp.zeros((rows, head_dim), BF16)
                        live[place, here, :] = jnp.zeros((rows, head_dim), BF16)

            return 0

        lax.fori_loop(0, holders, mend, 0)
        position = lax.broadcasted_iota(jnp.int32, (head_rows, head_dim), 0)
        admitted = position < split_ref[0] * rows
        keys, values = finish_head(width_total, gathered_ref, cos_ref, sin_ref)
        spare = blocks[full, :16, :head_dim].astype(F32)[:1]
        blocks[2 * holders, :head_rows, :head_dim] = jnp.where(admitted, keys, spare).astype(BF16)
        blocks[2 * holders, :head_rows, head_dim:] = jnp.where(admitted, values, 0.0).astype(BF16)
        live[2 * holders, :head_rows, :] = jnp.where(admitted, 1.0, 0.0).astype(BF16)

    heads = queries_ref.shape[1] // head_dim
    total_rows = queries_ref.shape[0]
    row = lax.broadcasted_iota(jnp.int32, (block, block), 0)
    column = lax.broadcasted_iota(jnp.int32, (block, block), 1)
    step = chunk // slab
    starts = list(range(0, 2 * holders, step))

    def doubled(keys):
        return jnp.concatenate([keys, keys], axis=1)

    for b in range(total_rows // block):
        here = pl.ds(b * block, block)
        query = [
            scaled_queries(queries_ref[here, h * head_dim : (h + 1) * head_dim], head_dim) for h in range(heads)
        ]
        state = [None] * heads
        for earlier in range(b + 1):
            there = pl.ds(earlier * block, block)
            keys = doubled(fresh_ref[there, :head_dim])
            values = fresh_ref[there, head_dim:]
            values = jnp.concatenate([values, jnp.ones_like(values)], axis=1)
            for h in range(heads):
                mask = column <= row if earlier == b else None
                state[h] = extend(state[h], query[h], keys, values, mask)
        if b == 0:
            gather_blocks()
        for start in starts:
            parts = list(range(start, start + step))
            taken = [blocks[i] for i in parts]
            weights = [live[i] for i in parts]
            if start == starts[-1]:
                taken.append(blocks[2 * holders, :head_rows])
                weights.append(live[2 * holders, :head_rows])
            taken = jnp.concatenate(taken, axis=0)
            values = jnp.concatenate([taken[:, head_dim:], jnp.concatenate(weights, axis=0)], axis=1)
            for h in range(heads):
                state[h] = extend(state[h], query[h], doubled(taken[:, :head_dim]), values)
        for h in range(heads):
            mixed = state[h][1]
            out_ref[here, h * head_dim : (h + 1) * head_dim] = (
                mixed[:, :head_dim] / mixed[:, head_dim:]
            ).astype(BF16)


def attend(counts, split, queries, fresh, own, other, gathered, width_total):
    rows, width = queries.shape
    holders, slab, pair = own.shape
    cosine, sine = rotation(gathered.shape[1] - EXTRA, pair // 2)
    anywhere = pl.BlockSpec(memory_space=pl.ANY)
    return pl.pallas_call(
        functools.partial(attend_kernel, min(512, rows), 512, width_total),
        in_specs=[SMEM, SMEM, VMEM, VMEM, anywhere, anywhere, VMEM, VMEM, VMEM],
        out_specs=VMEM,
        scratch_shapes=[
            pltpu.VMEM((2 * holders + 1, slab, pair), BF16),
            pltpu.VMEM((2 * holders + 1, slab, pair // 2), BF16),
            pltpu.SemaphoreType.DMA((2,)),
        ],
        out_shape=jax.ShapeDtypeStruct((rows, width), BF16),
        compiler_params=params(24),
        cost_estimate=pl.CostEstimate(flops=2**34, bytes_accessed=2**22, transcendentals=2**23),
        name="attend",
    )(counts, split, queries, fresh, own, other, gathered, cosine, sine)


def per_device(
    queries,
    fresh_kv,
    head_hidden,
    norm_gain,
    kv_weight,
    kv_store,
    split_blocks,
    tail_counts,
    holder_list,
    slot_list,
):
    holders = lax.axis_size(POOL)
    capacity = holder_list.shape[1] // holders
    packed, send, keep, counts = prepare(
        tail_counts,
        holder_list,
        slot_list,
        head_hidden[0],
        norm_gain,
        kv_weight,
        kv_store[:, :, 0, :],
        capacity // 2,
        holders,
        lax.axis_size("y"),
    )
    own = lax.all_to_all(packed, POOL, split_axis=0, concat_axis=0, tiled=True)
    turns = join_cores(lax.all_gather(send, "core", axis=0), keep)
    arrived = [lax.ppermute(turn, COMP, owners_of_turn(t)) for t, turn in enumerate(turns)]
    gathered = lax.all_gather(join_chips(arrived), QUAD, axis=0)
    own, gathered = lax.optimization_barrier((own, gathered))
    other = lax.ppermute(own, "core", SWAP)
    return attend(
        counts,
        split_blocks,
        queries[0],
        fresh_kv[0, :, 0, :],
        own,
        other,
        gathered,
        head_hidden.shape[2] * lax.axis_size(COMP),
    )[None]


def solution(mesh):
    fine = Mesh(mesh.devices.reshape(2, 8, 8, 2, 2), ("xh", "z", "y", "xl", "core"))
    return jax.shard_map(
        per_device,
        mesh=fine,
        in_specs=(
            P(POOL, None, COMP),
            P(POOL, None, COMP, None),
            P(POOL, None, COMP),
            P(COMP),
            P(COMP, None),
            P(POOL, None, COMP, None),
            P(POOL),
            P(),
            P(),
            P(),
        ),
        out_specs=P(POOL, None, COMP),
        check_vma=False,
    )
```

```python
import functools
import math

import jax
import jax.numpy as jnp
import numpy as np
from jax import lax
from jax.experimental import pallas as pl
from jax.experimental.pallas import tpu as pltpu
from jax.sharding import Mesh, PartitionSpec as P

F32 = jnp.float32
BF16 = jnp.bfloat16
NT = (((1,), (1,)), ((), ()))
LOW = -1e30
QUAD = ("xl", "core")
COMP = ("y", "xl", "core")
POOL = ("xh", "z")
SWAP = [(0, 1), (1, 0)]
SMEM = pl.BlockSpec(memory_space=pltpu.SMEM)
VMEM = pl.BlockSpec(memory_space=pltpu.VMEM)


def params(mebibytes):
    return pltpu.CompilerParams(vmem_limit_bytes=mebibytes * 2**20)


EXTRA = 16


def split_squares(total, rows):
    half = total.shape[1] // 2
    return total[:rows], total[rows:, :half] + total[rows:, half:]


def in_bfloat16(total, rows):
    main, squares = split_squares(total, rows)
    high = squares.astype(BF16)
    low = (squares - high.astype(F32)).astype(BF16)
    return jnp.concatenate([main.astype(BF16), jnp.concatenate([high, low], axis=1)], axis=0)


def block_counts(tail_ref, holder_ref, counts_ref):
    cells = holder_ref.shape[1]
    holders = counts_ref.shape[0]
    session = lax.axis_index("xh") * lax.axis_size("z") + lax.axis_index("z")
    holder = lax.broadcasted_iota(jnp.int32, (holders, cells), 0)
    cell = lax.broadcasted_iota(jnp.int32, (holders, cells), 1)
    match = (holder_ref[pl.ds(session, 1), :] == holder) & (cell < tail_ref[session])
    found = jnp.sum(jnp.where(match, 1.0, 0.0), axis=1, keepdims=True).astype(jnp.int32)
    lane = lax.broadcasted_iota(jnp.int32, counts_ref.shape, 1)
    counts = jnp.where(lane == 0, found, 0)
    counts_ref[...] = jnp.where(lane == 1, lax.axis_index("core"), counts)


def offsets(turn):
    return 3 - turn, turn - 4


def held_slots(share, tail_ref, holder_ref, slot_ref):
    sessions, cells = holder_ref.shape
    me = lax.axis_index("xh") * lax.axis_size("z") + lax.axis_index("z")
    core = lax.axis_index("core")
    row = lax.broadcasted_iota(jnp.int32, (sessions, cells), 0)
    cell = lax.broadcasted_iota(jnp.int32, (sessions, cells), 1)
    tails = jnp.zeros((sessions, cells), jnp.int32)
    for s in range(sessions):
        tails = jnp.where(row == s, tail_ref[s], tails)
    held = (holder_ref[...] == me) & (cell < tails)
    before = lax.broadcasted_iota(jnp.int32, (cells, cells), 0)
    until = lax.broadcasted_iota(jnp.int32, (cells, cells), 1)
    order = jnp.dot(
        jnp.where(held, 1.0, 0.0).astype(BF16),
        jnp.where(before <= until, 1.0, 0.0).astype(BF16),
        preferred_element_type=F32,
    )
    lane = lax.broadcasted_iota(jnp.int32, (sessions, 128), 1)
    slots = jnp.zeros((sessions, 128), jnp.int32)
    for k in range(share):
        wanted = (core * share + k + 1).astype(F32)
        pick = jnp.where(held & (order == wanted), slot_ref[...], 0)
        slots = jnp.where(lane == k, jnp.sum(pick, axis=1, keepdims=True), slots)
    return slots


def prepare_kernel(tail_ref, holder_ref, slot_ref, hidden_ref, gain_ref, weight_hbm, store_ref,
                   packed_ref, send_ref, keep_ref, counts_ref,
                   counts, staged, weight_ref, send, keep, sems, in_sems, out_sems):
    sessions = holder_ref.shape[0]
    block_rows = store_ref.shape[1]
    share = packed_ref.shape[1] // block_rows
    weight_copy = pltpu.make_async_copy(weight_hbm, weight_ref, sems.at[0])
    weight_copy.start()
    slots = held_slots(share, tail_ref, holder_ref, slot_ref)

    def block_in(s, k):
        return pltpu.make_async_copy(
            store_ref.at[slots[s, k]],
            staged.at[s, pl.ds(k * block_rows, block_rows)],
            in_sems.at[s * share + k],
        )

    def slab_out(s):
        return pltpu.make_async_copy(staged.at[s], packed_ref.at[s], out_sems.at[s])

    for s in range(sessions):
        for k in range(share):
            block_in(s, k).start()

    hidden = hidden_ref[...].astype(F32)
    rows = hidden.shape[0]
    width = send.shape[2]
    core = lax.axis_index("core")
    scaled = (hidden * gain_ref[...].astype(F32)[None, :]).astype(BF16)
    squares = lax.dot_general(
        jnp.ones((EXTRA, hidden.shape[1]), F32), hidden * hidden, NT,
        precision=lax.Precision.HIGHEST, preferred_element_type=F32,
    )
    weight_copy.wait()

    def partial_sums(t, side):
        head = lax.rem(lax.axis_index("y") + jnp.where(side == 0, *offsets(t)) + 8, 8)
        columns = pl.ds(pl.multiple_of(head * width, width), width)
        return jnp.dot(scaled, weight_ref[:, columns], preferred_element_type=F32)

    high = squares.astype(BF16)
    low = (squares - high.astype(F32)).astype(BF16)
    for t in range(4):
        send[t, :rows, :] = partial_sums(t, 1 - core).astype(BF16)
        send[t, rows:, :] = jnp.concatenate([high, low], axis=1)
    send_copy = pltpu.make_async_copy(send, send_ref, sems.at[2])
    send_copy.start()
    for t in range(4):
        keep[t, :rows, :] = partial_sums(t, core)
        keep[t, rows:, :] = jnp.concatenate([squares, jnp.zeros_like(squares)], axis=1)
    keep_copy = pltpu.make_async_copy(keep, keep_ref, sems.at[3])
    keep_copy.start()
    block_counts(tail_ref, holder_ref, counts)
    counts_copy = pltpu.make_async_copy(counts, counts_ref, sems.at[1])
    counts_copy.start()

    for s in range(sessions):
        for k in range(share):
            block_in(s, k).wait()
        slab_out(s).start()
    send_copy.wait()
    keep_copy.wait()
    counts_copy.wait()
    for s in range(sessions):
        slab_out(s).wait()


def prepare(tail_counts, holder_list, slot_list, hidden, gain, weight, store, share, holders, heads):
    sessions, cells = holder_list.shape
    _, block_rows, width = store.shape
    partials = (heads // 2, hidden.shape[0] + EXTRA, width)
    packed = (sessions, share * block_rows, width)
    anywhere = pl.BlockSpec(memory_space=pl.ANY)
    return pl.pallas_call(
        prepare_kernel,
        out_shape=(
            jax.ShapeDtypeStruct(packed, BF16),
            jax.ShapeDtypeStruct(partials, BF16),
            jax.ShapeDtypeStruct(partials, F32),
            jax.ShapeDtypeStruct((holders, 128), jnp.int32),
        ),
        in_specs=[SMEM, VMEM, VMEM, VMEM, VMEM, anywhere, anywhere],
        out_specs=(anywhere,) * 4,
        scratch_shapes=[
            pltpu.VMEM((holders, 128), jnp.int32),
            pltpu.VMEM(packed, BF16),
            pltpu.VMEM(weight.shape, BF16),
            pltpu.VMEM(partials, BF16),
            pltpu.VMEM(partials, F32),
            pltpu.SemaphoreType.DMA((4,)),
            pltpu.SemaphoreType.DMA((sessions * share,)),
            pltpu.SemaphoreType.DMA((sessions,)),
        ],
        compiler_params=params(56),
        name="prepare",
    )(tail_counts, holder_list, slot_list, hidden, gain, weight, store)


def join_cores_kernel(sent_ref, mine_ref, *out_refs):
    rows = mine_ref.shape[1] - EXTRA
    there = 1 - lax.axis_index("core")
    for t, out_ref in enumerate(out_refs):
        out_ref[...] = in_bfloat16(sent_ref[there, t].astype(F32) + mine_ref[t], rows)


def join_cores(sent, mine):
    out = jax.ShapeDtypeStruct(mine.shape[1:], BF16)
    return pl.pallas_call(
        join_cores_kernel, out_shape=(out,) * mine.shape[0], compiler_params=params(6), name="join_cores"
    )(sent, mine)


def join_chips_kernel(*refs):
    total = refs[0][...].astype(F32)
    for ref in refs[1:-1]:
        total = total + ref[...].astype(F32)
    refs[-1][...] = in_bfloat16(total, total.shape[0] - EXTRA)


def join_chips(arrived):
    return pl.pallas_call(
        join_chips_kernel,
        out_shape=jax.ShapeDtypeStruct(arrived[0].shape, BF16),
        compiler_params=params(6),
        name="join_chips",
    )(*arrived)


def owners_of_turn(turn):
    return [
        (y * 4 + 2 * xl + core, (y + offsets(turn)[core]) % 8 * 4 + 2 * xl + core)
        for y in range(8)
        for xl in range(2)
        for core in range(2)
    ]


def rotation(rows, head_dim):
    frequency = 500000.0 ** (-2.0 * np.arange(head_dim // 2) / head_dim)
    angles = np.arange(rows)[:, None] * frequency[None, :]
    cosine, sine = np.cos(angles), np.sin(angles)
    return (
        jnp.asarray(np.concatenate([cosine, cosine], axis=1), F32),
        jnp.asarray(np.concatenate([-sine, sine], axis=1), F32),
    )


def finish_head(width_total, gathered_ref, cos_ref, sin_ref):
    rows = gathered_ref.shape[1] - EXTRA
    half = gathered_ref.shape[2] // 2
    total = gathered_ref[0].astype(F32)
    for i in range(1, gathered_ref.shape[0]):
        total = total + gathered_ref[i].astype(F32)
    main, squares = split_squares(total, rows)
    lane = lax.broadcasted_iota(jnp.int32, (rows, half), 1)
    row = lax.broadcasted_iota(jnp.int32, (rows, half), 0)
    squares = jnp.sum(jnp.where(lane == row, squares[:1], 0.0), axis=1, keepdims=True)
    block = main * lax.rsqrt(squares / width_total + 1e-05)
    keys = block[:, :half]
    swapped = jnp.concatenate([keys[:, half // 2 :], keys[:, : half // 2]], axis=1)
    return keys * cos_ref[...] + swapped * sin_ref[...], block[:, half:]


def scaled_queries(queries, head_dim):
    scaled = queries.astype(F32) * (math.log2(math.e) / math.sqrt(head_dim))
    high = scaled.astype(BF16)
    low = (scaled - high.astype(F32)).astype(BF16)
    return jnp.concatenate([high, low], axis=1)


def extend(state, query, keys, values, mask=None):
    scores = lax.dot_general(query, keys, NT, preferred_element_type=F32)
    if mask is not None:
        scores = jnp.where(mask, scores, LOW)
    peak = jnp.max(scores, axis=1, keepdims=True)
    if state is not None:
        peak = jnp.maximum(peak, state[0])
    mixed = jnp.dot(jnp.exp2(scores - peak).astype(BF16), values, preferred_element_type=F32)
    if state is not None:
        mixed = mixed + state[1] * jnp.exp2(state[0] - peak)
    return peak, mixed


def doubled(keys):
    return jnp.concatenate([keys, keys], axis=1)


def block_queries(queries_ref, here, head_dim):
    return [
        scaled_queries(queries_ref[here, start : start + head_dim], head_dim)
        for start in range(0, queries_ref.shape[1], head_dim)
    ]


def fresh_kernel(block, queries_ref, fresh_ref, peak_ref, mixed_ref):
    head_dim = fresh_ref.shape[1] // 2
    row = lax.broadcasted_iota(jnp.int32, (block, block), 0)
    column = lax.broadcasted_iota(jnp.int32, (block, block), 1)
    for b in range(queries_ref.shape[0] // block):
        here = pl.ds(b * block, block)
        query = block_queries(queries_ref, here, head_dim)
        state = [None] * len(query)
        for earlier in range(b + 1):
            there = pl.ds(earlier * block, block)
            keys = doubled(fresh_ref[there, :head_dim])
            values = fresh_ref[there, head_dim:]
            values = jnp.concatenate([values, jnp.ones_like(values)], axis=1)
            for h in range(len(query)):
                state[h] = extend(state[h], query[h], keys, values, column <= row if earlier == b else None)
        for h, (peak, mixed) in enumerate(state):
            peak_ref[h, here, :] = jnp.broadcast_to(peak, (block, 128))
            mixed_ref[h, here, :] = mixed


def attend_fresh(queries, fresh):
    rows, width = queries.shape
    heads = 2 * width // fresh.shape[1]
    return pl.pallas_call(
        functools.partial(fresh_kernel, min(512, rows)),
        in_specs=[VMEM, VMEM],
        out_specs=(VMEM, VMEM),
        out_shape=(
            jax.ShapeDtypeStruct((heads, rows, 128), F32),
            jax.ShapeDtypeStruct((heads, rows, fresh.shape[1]), F32),
        ),
        compiler_params=params(24),
        cost_estimate=pl.CostEstimate(flops=2**31, bytes_accessed=2**21, transcendentals=2**20),
        name="attend_fresh",
    )(queries, fresh)


def attend_kernel(block, chunk, width_total, counts_ref, split_ref, queries_ref, fresh_ref, peak_ref, mixed_ref,
                  own_ref, other_ref, gathered_ref, cos_ref, sin_ref, out_ref, blocks, live, sems):
    holders, slab, width = own_ref.shape
    head_dim = width // 2
    head_rows = gathered_ref.shape[1] - EXTRA
    share = 2
    rows = slab // share
    core = counts_ref[0, 1]
    copies = [
        pltpu.make_async_copy(ref, blocks.at[pl.ds(side * holders, holders)], sems.at[side])
        for side, ref in enumerate((own_ref, other_ref))
    ]
    for copy in copies:
        copy.start()
    live[...] = jnp.ones(live.shape, BF16)
    spare = fresh_ref[:16, :head_dim].astype(F32)[:1]

    position = lax.broadcasted_iota(jnp.int32, (head_rows, head_dim), 0)
    admitted = position < jnp.reshape(split_ref[...], (1, 1)) * rows
    keys, values = finish_head(width_total, gathered_ref, cos_ref, sin_ref)
    head_keys = jnp.where(admitted, keys, spare).astype(BF16)
    head_values = jnp.where(admitted, values, 0.0).astype(BF16)
    head_live = jnp.where(admitted, 1.0, 0.0).astype(BF16)

    def mend(side):
        copies[side].wait()

        def mend_holder(holder, _):
            for k in range(share):

                @pl.when((core if side == 0 else 1 - core) * share + k >= counts_ref[holder, 0])
                def _():
                    here = pl.ds(k * rows, rows)
                    place = side * holders + holder
                    blocks[place, here, :head_dim] = jnp.broadcast_to(spare, (rows, head_dim)).astype(BF16)
                    blocks[place, here, head_dim:] = jnp.zeros((rows, head_dim), BF16)
                    live[place, here, :] = jnp.zeros((rows, head_dim), BF16)

            return 0

        lax.fori_loop(0, holders, mend_holder, 0)

    step = chunk // slab
    for b in range(queries_ref.shape[0] // block):
        here = pl.ds(b * block, block)
        query = block_queries(queries_ref, here, head_dim)
        state = [
            (jnp.max(peak_ref[h, here, :], axis=1, keepdims=True), mixed_ref[h, here, :])
            for h in range(len(query))
        ]
        for start in range(0, 2 * holders, step):
            if b == 0 and start % holders == 0:
                mend(start // holders)
            taken = jnp.concatenate([blocks[i] for i in range(start, start + step)], axis=0)
            keys, values = taken[:, :head_dim], taken[:, head_dim:]
            weights = jnp.concatenate([live[i] for i in range(start, start + step)], axis=0)
            if start == 0:
                keys = jnp.concatenate([head_keys, keys], axis=0)
                values = jnp.concatenate([head_values, values], axis=0)
                weights = jnp.concatenate([head_live, weights], axis=0)
            values = jnp.concatenate([values, weights], axis=1)
            for h in range(len(query)):
                state[h] = extend(state[h], query[h], doubled(keys), values)
        for h, (_, mixed) in enumerate(state):
            out_ref[here, h * head_dim : (h + 1) * head_dim] = (
                mixed[:, :head_dim] / mixed[:, head_dim:]
            ).astype(BF16)


def attend(counts, split, queries, fresh, peak, mixed, own, other, gathered, width_total):
    rows, width = queries.shape
    holders, slab, pair = own.shape
    cosine, sine = rotation(gathered.shape[1] - EXTRA, pair // 2)
    anywhere = pl.BlockSpec(memory_space=pl.ANY)
    return pl.pallas_call(
        functools.partial(attend_kernel, min(512, rows), 512, width_total),
        in_specs=[SMEM, VMEM, VMEM, VMEM, VMEM, VMEM, anywhere, anywhere, VMEM, VMEM, VMEM],
        out_specs=VMEM,
        scratch_shapes=[
            pltpu.VMEM((2 * holders, slab, pair), BF16),
            pltpu.VMEM((2 * holders, slab, pair // 2), BF16),
            pltpu.SemaphoreType.DMA((2,)),
        ],
        out_shape=jax.ShapeDtypeStruct((rows, width), BF16),
        compiler_params=params(24),
        cost_estimate=pl.CostEstimate(flops=2**34, bytes_accessed=2**22, transcendentals=2**23),
        name="attend",
    )(counts, split, queries, fresh, peak, mixed, own, other, gathered, cosine, sine)


def per_device(
    queries,
    fresh_kv,
    head_hidden,
    norm_gain,
    kv_weight,
    kv_store,
    split_blocks,
    tail_counts,
    holder_list,
    slot_list,
):
    holders = lax.axis_size(POOL)
    capacity = holder_list.shape[1] // holders
    packed, send, keep, counts = prepare(
        tail_counts,
        holder_list,
        slot_list,
        head_hidden[0],
        norm_gain,
        kv_weight,
        kv_store[:, :, 0, :],
        capacity // 2,
        holders,
        lax.axis_size("y"),
    )
    own = lax.all_to_all(packed, POOL, split_axis=0, concat_axis=0, tiled=True)
    turns = join_cores(lax.all_gather(send, "core", axis=0), keep)
    arrived = [lax.ppermute(turn, COMP, owners_of_turn(t)) for t, turn in enumerate(turns)]
    gathered = lax.all_gather(join_chips(arrived), QUAD, axis=0)
    own, gathered, queries = lax.optimization_barrier((own, gathered, queries))
    other = lax.ppermute(own, "core", SWAP)
    fresh = fresh_kv[0, :, 0, :]
    peak, mixed = attend_fresh(queries[0], fresh)
    return attend(
        counts,
        split_blocks,
        queries[0],
        fresh,
        peak,
        mixed,
        own,
        other,
        gathered,
        head_hidden.shape[2] * lax.axis_size(COMP),
    )[None]


def solution(mesh):
    fine = Mesh(mesh.devices.reshape(2, 8, 8, 2, 2), ("xh", "z", "y", "xl", "core"))
    return jax.shard_map(
        per_device,
        mesh=fine,
        in_specs=(
            P(POOL, None, COMP),
            P(POOL, None, COMP, None),
            P(POOL, None, COMP),
            P(COMP),
            P(COMP, None),
            P(POOL, None, COMP, None),
            P(POOL),
            P(),
            P(),
            P(),
        ),
        out_specs=P(POOL, None, COMP),
        check_vma=False,
    )
```

```python
import functools
import math

import jax
import jax.numpy as jnp
import numpy as np
from jax import lax
from jax.experimental import pallas as pl
from jax.experimental.pallas import tpu as pltpu
from jax.sharding import Mesh, PartitionSpec as P

F32 = jnp.float32
BF16 = jnp.bfloat16
NT = (((1,), (1,)), ((), ()))
LOW = -1e30
QUAD = ("xl", "core")
COMP = ("y", "xl", "core")
POOL = ("xh", "z")
SWAP = [(0, 1), (1, 0)]
SMEM = pl.BlockSpec(memory_space=pltpu.SMEM)
VMEM = pl.BlockSpec(memory_space=pltpu.VMEM)


def params(mebibytes):
    return pltpu.CompilerParams(vmem_limit_bytes=mebibytes * 2**20)


EXTRA = 16


def split_squares(total, rows):
    half = total.shape[1] // 2
    return total[:rows], total[rows:, :half] + total[rows:, half:]


def in_bfloat16(total, rows):
    main, squares = split_squares(total, rows)
    high = squares.astype(BF16)
    low = (squares - high.astype(F32)).astype(BF16)
    return jnp.concatenate([main.astype(BF16), jnp.concatenate([high, low], axis=1)], axis=0)


def block_counts(tail_ref, holder_ref, counts_ref):
    cells = holder_ref.shape[1]
    holders = counts_ref.shape[0]
    session = lax.axis_index("xh") * lax.axis_size("z") + lax.axis_index("z")
    holder = lax.broadcasted_iota(jnp.int32, (holders, cells), 0)
    cell = lax.broadcasted_iota(jnp.int32, (holders, cells), 1)
    match = (holder_ref[pl.ds(session, 1), :] == holder) & (cell < tail_ref[session])
    found = jnp.sum(jnp.where(match, 1.0, 0.0), axis=1, keepdims=True).astype(jnp.int32)
    lane = lax.broadcasted_iota(jnp.int32, counts_ref.shape, 1)
    counts = jnp.where(lane == 0, found, 0)
    counts_ref[...] = jnp.where(lane == 1, lax.axis_index("core"), counts)


def offsets(turn):
    return 3 - turn, turn - 4


def held_slots(share, tail_ref, holder_ref, slot_ref):
    sessions, cells = holder_ref.shape
    me = lax.axis_index("xh") * lax.axis_size("z") + lax.axis_index("z")
    core = lax.axis_index("core")
    row = lax.broadcasted_iota(jnp.int32, (sessions, cells), 0)
    cell = lax.broadcasted_iota(jnp.int32, (sessions, cells), 1)
    tails = jnp.zeros((sessions, cells), jnp.int32)
    for s in range(sessions):
        tails = jnp.where(row == s, tail_ref[s], tails)
    held = (holder_ref[...] == me) & (cell < tails)
    before = lax.broadcasted_iota(jnp.int32, (cells, cells), 0)
    until = lax.broadcasted_iota(jnp.int32, (cells, cells), 1)
    order = jnp.dot(
        jnp.where(held, 1.0, 0.0).astype(BF16),
        jnp.where(before <= until, 1.0, 0.0).astype(BF16),
        preferred_element_type=F32,
    )
    lane = lax.broadcasted_iota(jnp.int32, (sessions, 128), 1)
    slots = jnp.zeros((sessions, 128), jnp.int32)
    for k in range(share):
        wanted = (core * share + k + 1).astype(F32)
        pick = jnp.where(held & (order == wanted), slot_ref[...], 0)
        slots = jnp.where(lane == k, jnp.sum(pick, axis=1, keepdims=True), slots)
    return slots


def prepare_kernel(tail_ref, holder_ref, slot_ref, hidden_ref, gain_ref, weight_hbm, store_ref,
                   packed_ref, send_ref, keep_ref, counts_ref,
                   counts, staged, weight_ref, send, keep, sems, in_sems, out_sems):
    sessions = holder_ref.shape[0]
    block_rows = store_ref.shape[1]
    share = packed_ref.shape[1] // block_rows
    weight_copy = pltpu.make_async_copy(weight_hbm, weight_ref, sems.at[0])
    weight_copy.start()
    slots = held_slots(share, tail_ref, holder_ref, slot_ref)

    def block_in(s, k):
        return pltpu.make_async_copy(
            store_ref.at[slots[s, k]],
            staged.at[s, pl.ds(k * block_rows, block_rows)],
            in_sems.at[s * share + k],
        )

    def slab_out(s):
        return pltpu.make_async_copy(staged.at[s], packed_ref.at[s], out_sems.at[s])

    for s in range(sessions):
        for k in range(share):
            block_in(s, k).start()

    hidden = hidden_ref[...].astype(F32)
    rows = hidden.shape[0]
    width = send.shape[2]
    core = lax.axis_index("core")
    scaled = (hidden * gain_ref[...].astype(F32)[None, :]).astype(BF16)
    squares = lax.dot_general(
        jnp.ones((EXTRA, hidden.shape[1]), F32), hidden * hidden, NT,
        precision=lax.Precision.HIGHEST, preferred_element_type=F32,
    )
    weight_copy.wait()

    def partial_sums(t, side):
        head = lax.rem(lax.axis_index("y") + jnp.where(side == 0, *offsets(t)) + 8, 8)
        columns = pl.ds(pl.multiple_of(head * width, width), width)
        return jnp.dot(scaled, weight_ref[:, columns], preferred_element_type=F32)

    high = squares.astype(BF16)
    low = (squares - high.astype(F32)).astype(BF16)
    for t in range(4):
        send[t, :rows, :] = partial_sums(t, 1 - core).astype(BF16)
        send[t, rows:, :] = jnp.concatenate([high, low], axis=1)
    send_copy = pltpu.make_async_copy(send, send_ref, sems.at[2])
    send_copy.start()
    for t in range(4):
        keep[t, :rows, :] = partial_sums(t, core)
        keep[t, rows:, :] = jnp.concatenate([squares, jnp.zeros_like(squares)], axis=1)
    keep_copy = pltpu.make_async_copy(keep, keep_ref, sems.at[3])
    keep_copy.start()
    block_counts(tail_ref, holder_ref, counts)
    counts_copy = pltpu.make_async_copy(counts, counts_ref, sems.at[1])
    counts_copy.start()

    for s in range(sessions):
        for k in range(share):
            block_in(s, k).wait()
        slab_out(s).start()
    send_copy.wait()
    keep_copy.wait()
    counts_copy.wait()
    for s in range(sessions):
        slab_out(s).wait()


def prepare(tail_counts, holder_list, slot_list, hidden, gain, weight, store, share, holders, heads):
    sessions, cells = holder_list.shape
    _, block_rows, width = store.shape
    partials = (heads // 2, hidden.shape[0] + EXTRA, width)
    packed = (sessions, share * block_rows, width)
    anywhere = pl.BlockSpec(memory_space=pl.ANY)
    return pl.pallas_call(
        prepare_kernel,
        out_shape=(
            jax.ShapeDtypeStruct(packed, BF16),
            jax.ShapeDtypeStruct(partials, BF16),
            jax.ShapeDtypeStruct(partials, F32),
            jax.ShapeDtypeStruct((holders, 128), jnp.int32),
        ),
        in_specs=[SMEM, VMEM, VMEM, VMEM, VMEM, anywhere, anywhere],
        out_specs=(anywhere,) * 4,
        scratch_shapes=[
            pltpu.VMEM((holders, 128), jnp.int32),
            pltpu.VMEM(packed, BF16),
            pltpu.VMEM(weight.shape, BF16),
            pltpu.VMEM(partials, BF16),
            pltpu.VMEM(partials, F32),
            pltpu.SemaphoreType.DMA((4,)),
            pltpu.SemaphoreType.DMA((sessions * share,)),
            pltpu.SemaphoreType.DMA((sessions,)),
        ],
        compiler_params=params(56),
        name="prepare",
    )(tail_counts, holder_list, slot_list, hidden, gain, weight, store)


def join_cores_kernel(sent_ref, mine_ref, *out_refs):
    rows = mine_ref.shape[1] - EXTRA
    there = 1 - lax.axis_index("core")
    for t, out_ref in enumerate(out_refs):
        out_ref[...] = in_bfloat16(sent_ref[there, t].astype(F32) + mine_ref[t], rows)


def join_cores(sent, mine):
    out = jax.ShapeDtypeStruct(mine.shape[1:], BF16)
    return pl.pallas_call(
        join_cores_kernel, out_shape=(out,) * mine.shape[0], compiler_params=params(6), name="join_cores"
    )(sent, mine)


def join_chips_kernel(*refs):
    total = refs[0][...].astype(F32)
    for ref in refs[1:-1]:
        total = total + ref[...].astype(F32)
    refs[-1][...] = in_bfloat16(total, total.shape[0] - EXTRA)


def join_chips(arrived):
    return pl.pallas_call(
        join_chips_kernel,
        out_shape=jax.ShapeDtypeStruct(arrived[0].shape, BF16),
        compiler_params=params(6),
        name="join_chips",
    )(*arrived)


def owners_of_turn(turn):
    return [
        (y * 4 + 2 * xl + core, (y + offsets(turn)[core]) % 8 * 4 + 2 * xl + core)
        for y in range(8)
        for xl in range(2)
        for core in range(2)
    ]


def rotation(rows, head_dim):
    frequency = 500000.0 ** (-2.0 * np.arange(head_dim // 2) / head_dim)
    angles = np.arange(rows)[:, None] * frequency[None, :]
    cosine, sine = np.cos(angles), np.sin(angles)
    return (
        jnp.asarray(np.concatenate([cosine, cosine], axis=1), F32),
        jnp.asarray(np.concatenate([-sine, sine], axis=1), F32),
    )


def finish_head(width_total, gathered_ref, cos_ref, sin_ref):
    rows = gathered_ref.shape[1] - EXTRA
    half = gathered_ref.shape[2] // 2
    total = gathered_ref[0].astype(F32)
    for i in range(1, gathered_ref.shape[0]):
        total = total + gathered_ref[i].astype(F32)
    main, squares = split_squares(total, rows)
    lane = lax.broadcasted_iota(jnp.int32, (rows, half), 1)
    row = lax.broadcasted_iota(jnp.int32, (rows, half), 0)
    squares = jnp.sum(jnp.where(lane == row, squares[:1], 0.0), axis=1, keepdims=True)
    block = main * lax.rsqrt(squares / width_total + 1e-05)
    keys = block[:, :half]
    swapped = jnp.concatenate([keys[:, half // 2 :], keys[:, : half // 2]], axis=1)
    return keys * cos_ref[...] + swapped * sin_ref[...], block[:, half:]


def scaled_queries(queries, head_dim):
    scaled = queries.astype(F32) * (math.log2(math.e) / math.sqrt(head_dim))
    high = scaled.astype(BF16)
    low = (scaled - high.astype(F32)).astype(BF16)
    return jnp.concatenate([high, low], axis=1)


def extend(state, query, keys, values, mask=None):
    scores = lax.dot_general(query, keys, NT, preferred_element_type=F32)
    if mask is not None:
        scores = jnp.where(mask, scores, LOW)
    peak = jnp.max(scores, axis=1, keepdims=True)
    if state is not None:
        peak = jnp.maximum(peak, state[0])
    mixed = jnp.dot(jnp.exp2(scores - peak).astype(BF16), values, preferred_element_type=F32)
    if state is not None:
        mixed = mixed + state[1] * jnp.exp2(state[0] - peak)
    return peak, mixed


def doubled(keys):
    return jnp.concatenate([keys, keys], axis=1)


def block_queries(queries_ref, here, head_dim):
    return [
        scaled_queries(queries_ref[here, start : start + head_dim], head_dim)
        for start in range(0, queries_ref.shape[1], head_dim)
    ]


def fresh_kernel(block, queries_ref, fresh_ref, peak_ref, mixed_ref):
    head_dim = fresh_ref.shape[1] // 2
    row = lax.broadcasted_iota(jnp.int32, (block, block), 0)
    column = lax.broadcasted_iota(jnp.int32, (block, block), 1)
    for b in range(queries_ref.shape[0] // block):
        here = pl.ds(b * block, block)
        query = block_queries(queries_ref, here, head_dim)
        state = [None] * len(query)
        for earlier in range(b + 1):
            there = pl.ds(earlier * block, block)
            keys = doubled(fresh_ref[there, :head_dim])
            values = fresh_ref[there, head_dim:]
            values = jnp.concatenate([values, jnp.ones_like(values)], axis=1)
            for h in range(len(query)):
                state[h] = extend(state[h], query[h], keys, values, column <= row if earlier == b else None)
        for h, (peak, mixed) in enumerate(state):
            peak_ref[h, here, :] = jnp.broadcast_to(peak, (block, 128))
            mixed_ref[h, here, :] = mixed


def attend_fresh(queries, fresh):
    rows, width = queries.shape
    heads = 2 * width // fresh.shape[1]
    return pl.pallas_call(
        functools.partial(fresh_kernel, min(512, rows)),
        in_specs=[VMEM, VMEM],
        out_specs=(VMEM, VMEM),
        out_shape=(
            jax.ShapeDtypeStruct((heads, rows, 128), F32),
            jax.ShapeDtypeStruct((heads, rows, fresh.shape[1]), F32),
        ),
        compiler_params=params(24),
        cost_estimate=pl.CostEstimate(flops=2**31, bytes_accessed=2**21, transcendentals=2**20),
        name="attend_fresh",
    )(queries, fresh)


def attend_kernel(block, chunk, width_total, counts_ref, split_ref, queries_ref, fresh_ref, peak_ref, mixed_ref,
                  own_ref, other_ref, gathered_ref, cos_ref, sin_ref, out_ref):
    holders, slab, width = own_ref.shape
    head_dim = width // 2
    head_rows = gathered_ref.shape[1] - EXTRA
    share = 2
    rows = slab // share
    core = counts_ref[0, 1]
    spare = fresh_ref[:16, :head_dim].astype(F32)[:1]
    spare_block = jnp.broadcast_to(spare, (rows, head_dim)).astype(BF16)

    position = lax.broadcasted_iota(jnp.int32, (head_rows, head_dim), 0)
    admitted = position < jnp.reshape(split_ref[...], (1, 1)) * rows
    keys, values = finish_head(width_total, gathered_ref, cos_ref, sin_ref)
    head_keys = jnp.where(admitted, keys, spare).astype(BF16)
    head_values = jnp.where(admitted, values, 0.0).astype(BF16)
    head_live = jnp.where(admitted, 1.0, 0.0).astype(BF16)

    def admitted_rows(side, first, last):
        ref = own_ref if side == 0 else other_ref
        first_slot = (core if side == 0 else 1 - core) * share
        keys, values, weights = [], [], []
        for holder in range(first, last):
            for k in range(share):
                weight = jnp.where(first_slot + k < counts_ref[holder, 0], 1.0, 0.0)
                piece = ref[holder, k * rows : (k + 1) * rows, :]
                keys.append(
                    piece[:, :head_dim] * weight.astype(BF16) + spare_block * (1.0 - weight).astype(BF16)
                )
                values.append(piece[:, head_dim:] * weight.astype(BF16))
                weights.append(jnp.full((rows, head_dim), weight, F32).astype(BF16))
        return [jnp.concatenate(parts, axis=0) for parts in (keys, values, weights)]

    step = chunk // slab
    for b in range(queries_ref.shape[0] // block):
        here = pl.ds(b * block, block)
        query = block_queries(queries_ref, here, head_dim)
        state = [
            (jnp.max(peak_ref[h, here, :], axis=1, keepdims=True), mixed_ref[h, here, :])
            for h in range(len(query))
        ]
        for start in range(0, 2 * holders, step):
            first = start % holders
            keys, values, weights = admitted_rows(start // holders, first, first + step)
            if start == 0:
                keys = jnp.concatenate([head_keys, keys], axis=0)
                values = jnp.concatenate([head_values, values], axis=0)
                weights = jnp.concatenate([head_live, weights], axis=0)
            values = jnp.concatenate([values, weights], axis=1)
            for h in range(len(query)):
                state[h] = extend(state[h], query[h], doubled(keys), values)
        for h, (_, mixed) in enumerate(state):
            out_ref[here, h * head_dim : (h + 1) * head_dim] = (
                mixed[:, :head_dim] / mixed[:, head_dim:]
            ).astype(BF16)


def attend(counts, split, queries, fresh, peak, mixed, own, other, gathered, width_total):
    rows, width = queries.shape
    holders, slab, pair = own.shape
    cosine, sine = rotation(gathered.shape[1] - EXTRA, pair // 2)
    return pl.pallas_call(
        functools.partial(attend_kernel, min(1024, rows), 256, width_total),
        in_specs=[SMEM] + [VMEM] * 10,
        out_specs=VMEM,
        out_shape=jax.ShapeDtypeStruct((rows, width), BF16),
        compiler_params=params(24),
        cost_estimate=pl.CostEstimate(flops=2**34, bytes_accessed=2**22, transcendentals=2**23),
        name="attend",
    )(counts, split, queries, fresh, peak, mixed, own, other, gathered, cosine, sine)


def per_device(
    queries,
    fresh_kv,
    head_hidden,
    norm_gain,
    kv_weight,
    kv_store,
    split_blocks,
    tail_counts,
    holder_list,
    slot_list,
):
    holders = lax.axis_size(POOL)
    capacity = holder_list.shape[1] // holders
    packed, send, keep, counts = prepare(
        tail_counts,
        holder_list,
        slot_list,
        head_hidden[0],
        norm_gain,
        kv_weight,
        kv_store[:, :, 0, :],
        capacity // 2,
        holders,
        lax.axis_size("y"),
    )
    own = lax.all_to_all(packed, POOL, split_axis=0, concat_axis=0, tiled=True)
    turns = join_cores(lax.all_gather(send, "core", axis=0), keep)
    arrived = [lax.ppermute(turn, COMP, owners_of_turn(t)) for t, turn in enumerate(turns)]
    gathered = lax.all_gather(join_chips(arrived), QUAD, axis=0)
    own, gathered, queries = lax.optimization_barrier((own, gathered, queries))
    other = lax.ppermute(own, "core", SWAP)
    fresh = fresh_kv[0, :, 0, :]
    peak, mixed = attend_fresh(queries[0], fresh)
    return attend(
        counts,
        split_blocks,
        queries[0],
        fresh,
        peak,
        mixed,
        own,
        other,
        gathered,
        head_hidden.shape[2] * lax.axis_size(COMP),
    )[None]


def solution(mesh):
    fine = Mesh(mesh.devices.reshape(2, 8, 8, 2, 2), ("xh", "z", "y", "xl", "core"))
    return jax.shard_map(
        per_device,
        mesh=fine,
        in_specs=(
            P(POOL, None, COMP),
            P(POOL, None, COMP, None),
            P(POOL, None, COMP),
            P(COMP),
            P(COMP, None),
            P(POOL, None, COMP, None),
            P(POOL),
            P(),
            P(),
            P(),
        ),
        out_specs=P(POOL, None, COMP),
        check_vma=False,
    )
```

```python
import functools
import math

import jax
import jax.numpy as jnp
import numpy as np
from jax import lax
from jax.experimental import pallas as pl
from jax.experimental.pallas import tpu as pltpu
from jax.sharding import Mesh, PartitionSpec as P

F32 = jnp.float32
BF16 = jnp.bfloat16
NT = (((1,), (1,)), ((), ()))
LOW = -1e30
QUAD = ("xl", "core")
COMP = ("y", "xl", "core")
POOL = ("xh", "z")
SWAP = [(0, 1), (1, 0)]
SMEM = pl.BlockSpec(memory_space=pltpu.SMEM)
VMEM = pl.BlockSpec(memory_space=pltpu.VMEM)


def params(mebibytes):
    return pltpu.CompilerParams(vmem_limit_bytes=mebibytes * 2**20)


EXTRA = 16


def split_squares(total, rows):
    half = total.shape[1] // 2
    return total[:rows], total[rows:, :half] + total[rows:, half:]


def in_bfloat16(total, rows):
    main, squares = split_squares(total, rows)
    high = squares.astype(BF16)
    low = (squares - high.astype(F32)).astype(BF16)
    return jnp.concatenate([main.astype(BF16), jnp.concatenate([high, low], axis=1)], axis=0)


def block_counts(tail_ref, holder_ref, counts_ref):
    cells = holder_ref.shape[1]
    holders = counts_ref.shape[0]
    session = lax.axis_index("xh") * lax.axis_size("z") + lax.axis_index("z")
    holder = lax.broadcasted_iota(jnp.int32, (holders, cells), 0)
    cell = lax.broadcasted_iota(jnp.int32, (holders, cells), 1)
    match = (holder_ref[pl.ds(session, 1), :] == holder) & (cell < tail_ref[session])
    found = jnp.sum(jnp.where(match, 1.0, 0.0), axis=1, keepdims=True).astype(jnp.int32)
    lane = lax.broadcasted_iota(jnp.int32, counts_ref.shape, 1)
    counts = jnp.where(lane == 0, found, 0)
    counts_ref[...] = jnp.where(lane == 1, lax.axis_index("core"), counts)


def offsets(turn):
    return 3 - turn, turn - 4


def held_slots(share, tail_ref, holder_ref, slot_ref):
    sessions, cells = holder_ref.shape
    me = lax.axis_index("xh") * lax.axis_size("z") + lax.axis_index("z")
    core = lax.axis_index("core")
    row = lax.broadcasted_iota(jnp.int32, (sessions, cells), 0)
    cell = lax.broadcasted_iota(jnp.int32, (sessions, cells), 1)
    tails = jnp.zeros((sessions, cells), jnp.int32)
    for s in range(sessions):
        tails = jnp.where(row == s, tail_ref[s], tails)
    held = (holder_ref[...] == me) & (cell < tails)
    before = lax.broadcasted_iota(jnp.int32, (cells, cells), 0)
    until = lax.broadcasted_iota(jnp.int32, (cells, cells), 1)
    order = jnp.dot(
        jnp.where(held, 1.0, 0.0).astype(BF16),
        jnp.where(before <= until, 1.0, 0.0).astype(BF16),
        preferred_element_type=F32,
    )
    lane = lax.broadcasted_iota(jnp.int32, (sessions, 128), 1)
    slots = jnp.zeros((sessions, 128), jnp.int32)
    for k in range(share):
        wanted = (core * share + k + 1).astype(F32)
        pick = jnp.where(held & (order == wanted), slot_ref[...], 0)
        slots = jnp.where(lane == k, jnp.sum(pick, axis=1, keepdims=True), slots)
    return slots


def prepare_kernel(tail_ref, holder_ref, slot_ref, hidden_ref, gain_ref, weight_hbm, store_ref,
                   packed_ref, send_ref, keep_ref, counts_ref,
                   counts, staged, weight_ref, send, keep, sems, in_sems, out_sems):
    sessions = holder_ref.shape[0]
    block_rows = store_ref.shape[1]
    share = packed_ref.shape[1] // block_rows
    weight_copy = pltpu.make_async_copy(weight_hbm, weight_ref, sems.at[0])
    weight_copy.start()
    slots = held_slots(share, tail_ref, holder_ref, slot_ref)

    def block_in(s, k):
        return pltpu.make_async_copy(
            store_ref.at[slots[s, k]],
            staged.at[s, pl.ds(k * block_rows, block_rows)],
            in_sems.at[s * share + k],
        )

    def slab_out(s):
        return pltpu.make_async_copy(staged.at[s], packed_ref.at[s], out_sems.at[s])

    for s in range(sessions):
        for k in range(share):
            block_in(s, k).start()

    hidden = hidden_ref[...].astype(F32)
    rows = hidden.shape[0]
    width = send.shape[2]
    core = lax.axis_index("core")
    scaled = (hidden * gain_ref[...].astype(F32)[None, :]).astype(BF16)
    squares = lax.dot_general(
        jnp.ones((EXTRA, hidden.shape[1]), F32), hidden * hidden, NT,
        precision=lax.Precision.HIGHEST, preferred_element_type=F32,
    )
    weight_copy.wait()

    def partial_sums(t, side):
        head = lax.rem(lax.axis_index("y") + jnp.where(side == 0, *offsets(t)) + 8, 8)
        columns = pl.ds(pl.multiple_of(head * width, width), width)
        return jnp.dot(scaled, weight_ref[:, columns], preferred_element_type=F32)

    high = squares.astype(BF16)
    low = (squares - high.astype(F32)).astype(BF16)
    for t in range(4):
        send[t, :rows, :] = partial_sums(t, 1 - core).astype(BF16)
        send[t, rows:, :] = jnp.concatenate([high, low], axis=1)
    send_copy = pltpu.make_async_copy(send, send_ref, sems.at[2])
    send_copy.start()
    for t in range(4):
        keep[t, :rows, :] = partial_sums(t, core)
        keep[t, rows:, :] = jnp.concatenate([squares, jnp.zeros_like(squares)], axis=1)
    keep_copy = pltpu.make_async_copy(keep, keep_ref, sems.at[3])
    keep_copy.start()
    block_counts(tail_ref, holder_ref, counts)
    counts_copy = pltpu.make_async_copy(counts, counts_ref, sems.at[1])
    counts_copy.start()

    for s in range(sessions):
        for k in range(share):
            block_in(s, k).wait()
        slab_out(s).start()
    send_copy.wait()
    keep_copy.wait()
    counts_copy.wait()
    for s in range(sessions):
        slab_out(s).wait()


def prepare(tail_counts, holder_list, slot_list, hidden, gain, weight, store, share, holders, heads):
    sessions, cells = holder_list.shape
    _, block_rows, width = store.shape
    partials = (heads // 2, hidden.shape[0] + EXTRA, width)
    packed = (sessions, share * block_rows, width)
    anywhere = pl.BlockSpec(memory_space=pl.ANY)
    return pl.pallas_call(
        prepare_kernel,
        out_shape=(
            jax.ShapeDtypeStruct(packed, BF16),
            jax.ShapeDtypeStruct(partials, BF16),
            jax.ShapeDtypeStruct(partials, F32),
            jax.ShapeDtypeStruct((holders, 128), jnp.int32),
        ),
        in_specs=[SMEM, VMEM, VMEM, VMEM, VMEM, anywhere, anywhere],
        out_specs=(anywhere,) * 4,
        scratch_shapes=[
            pltpu.VMEM((holders, 128), jnp.int32),
            pltpu.VMEM(packed, BF16),
            pltpu.VMEM(weight.shape, BF16),
            pltpu.VMEM(partials, BF16),
            pltpu.VMEM(partials, F32),
            pltpu.SemaphoreType.DMA((4,)),
            pltpu.SemaphoreType.DMA((sessions * share,)),
            pltpu.SemaphoreType.DMA((sessions,)),
        ],
        compiler_params=params(56),
        name="prepare",
    )(tail_counts, holder_list, slot_list, hidden, gain, weight, store)


def join_cores_kernel(sent_ref, mine_ref, *out_refs):
    rows = mine_ref.shape[1] - EXTRA
    there = 1 - lax.axis_index("core")
    for t, out_ref in enumerate(out_refs):
        out_ref[...] = in_bfloat16(sent_ref[there, t].astype(F32) + mine_ref[t], rows)


def join_cores(sent, mine):
    out = jax.ShapeDtypeStruct(mine.shape[1:], BF16)
    return pl.pallas_call(
        join_cores_kernel, out_shape=(out,) * mine.shape[0], compiler_params=params(6), name="join_cores"
    )(sent, mine)


def join_chips_kernel(*refs):
    total = refs[0][...].astype(F32)
    for ref in refs[1:-1]:
        total = total + ref[...].astype(F32)
    refs[-1][...] = in_bfloat16(total, total.shape[0] - EXTRA)


def join_chips(arrived):
    return pl.pallas_call(
        join_chips_kernel,
        out_shape=jax.ShapeDtypeStruct(arrived[0].shape, BF16),
        compiler_params=params(6),
        name="join_chips",
    )(*arrived)


def owners_of_turn(turn):
    return [
        (y * 4 + 2 * xl + core, (y + offsets(turn)[core]) % 8 * 4 + 2 * xl + core)
        for y in range(8)
        for xl in range(2)
        for core in range(2)
    ]


def rotation(rows, head_dim):
    frequency = 500000.0 ** (-2.0 * np.arange(head_dim // 2) / head_dim)
    angles = np.arange(rows)[:, None] * frequency[None, :]
    cosine, sine = np.cos(angles), np.sin(angles)
    return (
        jnp.asarray(np.concatenate([cosine, cosine], axis=1), F32),
        jnp.asarray(np.concatenate([-sine, sine], axis=1), F32),
    )


def finish_head(width_total, gathered_ref, cos_ref, sin_ref):
    rows = gathered_ref.shape[1] - EXTRA
    half = gathered_ref.shape[2] // 2
    total = gathered_ref[0].astype(F32)
    for i in range(1, gathered_ref.shape[0]):
        total = total + gathered_ref[i].astype(F32)
    main, squares = split_squares(total, rows)
    lane = lax.broadcasted_iota(jnp.int32, (rows, half), 1)
    row = lax.broadcasted_iota(jnp.int32, (rows, half), 0)
    squares = jnp.sum(jnp.where(lane == row, squares[:1], 0.0), axis=1, keepdims=True)
    block = main * lax.rsqrt(squares / width_total + 1e-05)
    keys = block[:, :half]
    swapped = jnp.concatenate([keys[:, half // 2 :], keys[:, : half // 2]], axis=1)
    return keys * cos_ref[...] + swapped * sin_ref[...], block[:, half:]


def scaled_queries(queries, head_dim):
    scaled = queries.astype(F32) * (math.log2(math.e) / math.sqrt(head_dim))
    high = scaled.astype(BF16)
    low = (scaled - high.astype(F32)).astype(BF16)
    return jnp.concatenate([high, low], axis=1)


def extend(state, query, keys, values, mask=None):
    scores = lax.dot_general(query, keys, NT, preferred_element_type=F32)
    if mask is not None:
        scores = jnp.where(mask, scores, LOW)
    peak = jnp.max(scores, axis=1, keepdims=True)
    if state is not None:
        peak = jnp.maximum(peak, state[0])
    mixed = jnp.dot(jnp.exp2(scores - peak).astype(BF16), values, preferred_element_type=F32)
    if state is not None:
        mixed = mixed + state[1] * jnp.exp2(state[0] - peak)
    return peak, mixed


def doubled(keys):
    return jnp.concatenate([keys, keys], axis=1)


def block_queries(queries_ref, here, head_dim):
    return [
        scaled_queries(queries_ref[here, start : start + head_dim], head_dim)
        for start in range(0, queries_ref.shape[1], head_dim)
    ]


def fresh_kernel(block, queries_ref, fresh_ref, peak_ref, mixed_ref):
    head_dim = fresh_ref.shape[1] // 2
    row = lax.broadcasted_iota(jnp.int32, (block, block), 0)
    column = lax.broadcasted_iota(jnp.int32, (block, block), 1)
    for b in range(queries_ref.shape[0] // block):
        here = pl.ds(b * block, block)
        query = block_queries(queries_ref, here, head_dim)
        state = [None] * len(query)
        for earlier in range(b + 1):
            there = pl.ds(earlier * block, block)
            keys = doubled(fresh_ref[there, :head_dim])
            values = fresh_ref[there, head_dim:]
            values = jnp.concatenate([values, jnp.ones_like(values)], axis=1)
            for h in range(len(query)):
                state[h] = extend(state[h], query[h], keys, values, column <= row if earlier == b else None)
        for h, (peak, mixed) in enumerate(state):
            peak_ref[h, here, :] = jnp.broadcast_to(peak, (block, 128))
            mixed_ref[h, here, :] = mixed


def attend_fresh(queries, fresh):
    rows, width = queries.shape
    heads = 2 * width // fresh.shape[1]
    return pl.pallas_call(
        functools.partial(fresh_kernel, min(256, rows)),
        in_specs=[VMEM, VMEM],
        out_specs=(VMEM, VMEM),
        out_shape=(
            jax.ShapeDtypeStruct((heads, rows, 128), F32),
            jax.ShapeDtypeStruct((heads, rows, fresh.shape[1]), F32),
        ),
        compiler_params=params(24),
        cost_estimate=pl.CostEstimate(flops=2**31, bytes_accessed=2**21, transcendentals=2**20),
        name="attend_fresh",
    )(queries, fresh)


def attend_kernel(block, chunk, width_total, counts_ref, split_ref, queries_ref, fresh_ref, peak_ref, mixed_ref,
                  own_ref, other_ref, gathered_ref, cos_ref, sin_ref, out_ref):
    holders, slab, width = own_ref.shape
    head_dim = width // 2
    head_rows = gathered_ref.shape[1] - EXTRA
    share = 2
    rows = slab // share
    core = counts_ref[0, 1]
    spare = fresh_ref[:16, :head_dim].astype(F32)[:1]
    spare_block = jnp.broadcast_to(spare, (rows, head_dim)).astype(BF16)

    position = lax.broadcasted_iota(jnp.int32, (head_rows, head_dim), 0)
    admitted = position < jnp.reshape(split_ref[...], (1, 1)) * rows
    keys, values = finish_head(width_total, gathered_ref, cos_ref, sin_ref)
    head_keys = jnp.where(admitted, keys, spare).astype(BF16)
    head_values = jnp.where(admitted, values, 0.0).astype(BF16)
    head_live = jnp.where(admitted, 1.0, 0.0).astype(BF16)

    def admitted_rows(side, first, last):
        ref = own_ref if side == 0 else other_ref
        first_slot = (core if side == 0 else 1 - core) * share
        keys, values, weights = [], [], []
        for holder in range(first, last):
            for k in range(share):
                weight = jnp.where(first_slot + k < counts_ref[holder, 0], 1.0, 0.0)
                piece = ref[holder, k * rows : (k + 1) * rows, :]
                keys.append(
                    piece[:, :head_dim] * weight.astype(BF16) + spare_block * (1.0 - weight).astype(BF16)
                )
                values.append(piece[:, head_dim:] * weight.astype(BF16))
                weights.append(jnp.full((rows, head_dim), weight, F32).astype(BF16))
        return [jnp.concatenate(parts, axis=0) for parts in (keys, values, weights)]

    step = chunk // slab
    for b in range(queries_ref.shape[0] // block):
        here = pl.ds(b * block, block)
        query = block_queries(queries_ref, here, head_dim)
        state = [
            (jnp.max(peak_ref[h, here, :], axis=1, keepdims=True), mixed_ref[h, here, :])
            for h in range(len(query))
        ]
        for start in range(0, 2 * holders, step):
            first = start % holders
            keys, values, weights = admitted_rows(start // holders, first, first + step)
            if start == 0:
                keys = jnp.concatenate([head_keys, keys], axis=0)
                values = jnp.concatenate([head_values, values], axis=0)
                weights = jnp.concatenate([head_live, weights], axis=0)
            values = jnp.concatenate([values, weights], axis=1)
            for h in range(len(query)):
                state[h] = extend(state[h], query[h], doubled(keys), values)
        for h, (_, mixed) in enumerate(state):
            out_ref[here, h * head_dim : (h + 1) * head_dim] = (
                mixed[:, :head_dim] / mixed[:, head_dim:]
            ).astype(BF16)


def attend(counts, split, queries, fresh, peak, mixed, own, other, gathered, width_total):
    rows, width = queries.shape
    holders, slab, pair = own.shape
    cosine, sine = rotation(gathered.shape[1] - EXTRA, pair // 2)
    return pl.pallas_call(
        functools.partial(attend_kernel, min(1024, rows), 256, width_total),
        in_specs=[SMEM] + [VMEM] * 10,
        out_specs=VMEM,
        out_shape=jax.ShapeDtypeStruct((rows, width), BF16),
        compiler_params=params(24),
        cost_estimate=pl.CostEstimate(flops=2**34, bytes_accessed=2**22, transcendentals=2**23),
        name="attend",
    )(counts, split, queries, fresh, peak, mixed, own, other, gathered, cosine, sine)


def per_device(
    queries,
    fresh_kv,
    head_hidden,
    norm_gain,
    kv_weight,
    kv_store,
    split_blocks,
    tail_counts,
    holder_list,
    slot_list,
):
    holders = lax.axis_size(POOL)
    capacity = holder_list.shape[1] // holders
    packed, send, keep, counts = prepare(
        tail_counts,
        holder_list,
        slot_list,
        head_hidden[0],
        norm_gain,
        kv_weight,
        kv_store[:, :, 0, :],
        capacity // 2,
        holders,
        lax.axis_size("y"),
    )
    own = lax.all_to_all(packed, POOL, split_axis=0, concat_axis=0, tiled=True)
    turns = join_cores(lax.all_gather(send, "core", axis=0), keep)
    arrived = [lax.ppermute(turn, COMP, owners_of_turn(t)) for t, turn in enumerate(turns)]
    gathered = lax.all_gather(join_chips(arrived), QUAD, axis=0)
    own, gathered, queries = lax.optimization_barrier((own, gathered, queries))
    other = lax.ppermute(own, "core", SWAP)
    fresh = fresh_kv[0, :, 0, :]
    peak, mixed = attend_fresh(queries[0], fresh)
    return attend(
        counts,
        split_blocks,
        queries[0],
        fresh,
        peak,
        mixed,
        own,
        other,
        gathered,
        head_hidden.shape[2] * lax.axis_size(COMP),
    )[None]


def solution(mesh):
    fine = Mesh(mesh.devices.reshape(2, 8, 8, 2, 2), ("xh", "z", "y", "xl", "core"))
    return jax.shard_map(
        per_device,
        mesh=fine,
        in_specs=(
            P(POOL, None, COMP),
            P(POOL, None, COMP, None),
            P(POOL, None, COMP),
            P(COMP),
            P(COMP, None),
            P(POOL, None, COMP, None),
            P(POOL),
            P(),
            P(),
            P(),
        ),
        out_specs=P(POOL, None, COMP),
        check_vma=False,
    )
```
